32 devices in a mesh: view: 4 (over x, core), dp: 8 (over z, y).
Axes of the slice: x: 2, y: 2, z: 4, core: 2. Of those that a mesh axis runs over, the one named last changes fastest.
Arguments:
- tokens: bfloat16 [4, 10368, 768], P('view', 'dp'), may hold values from -6 to 6
- item_class: int32 [32], P('dp'), may hold values from 0 to 2, as said below
- norm_gain: float32 [4, 3, 768], P('view'), may hold values from 0.5 to 1.5
- norm_bias: float32 [4, 3, 768], P('view'), may hold values from -1.75 to 1.75
- attn_qkv: bfloat16 [4, 768, 2304], P('view'), may hold values from -0.21875 to 0.21875
- attn_out: bfloat16 [4, 768, 768], P('view'), may hold values from -0.875 to 0.875
- mlp_up: bfloat16 [4, 768, 3072], P('view'), may hold values from -0.21875 to 0.21875
- mlp_down: bfloat16 [4, 3072, 768], P('view'), may hold values from -0.109375 to 0.109375
- join_query: bfloat16 [4, 768, 768], P('view'), may hold values from -0.21875 to 0.21875
- join_keyval: bfloat16 [4, 768, 1536], P('view'), may hold values from -0.21875 to 0.21875
- join_output: bfloat16 [4, 768, 768], P('view'), may hold values from -0.875 to 0.875
- cotangent: bfloat16 [4, 10368, 768], P('view', 'dp'), may hold values from -6 to 6
Outputs:
- joined_tokens: bfloat16 [4, 10368, 768], P('view', 'dp')
- grad_tokens: float32 [4, 10368, 768], P('view', 'dp')
- grad_norm_gain: float32 [4, 3, 768], P('view', None, 'dp')
- grad_norm_bias: float32 [4, 3, 768], P('view', None, 'dp')
- grad_attn_qkv: float32 [4, 768, 2304], P('view', 'dp')
- grad_attn_out: float32 [4, 768, 768], P('view', 'dp')
- grad_mlp_up: float32 [4, 768, 3072], P('view', 'dp')
- grad_mlp_down: float32 [4, 3072, 768], P('view', 'dp')
- grad_join_query: float32 [4, 768, 768], P('view', 'dp')
- grad_join_keyval: float32 [4, 768, 1536], P('view', 'dp')
- grad_join_output: float32 [4, 768, 768], P('view', 'dp')
The draws below stay inside these ranges and needn't reach their ends.
Inputs may be any that keep to these rules, and one draw needn't show every extreme that they name: `item_class`: each clip's resolution class; class 2 and class 0 both occur in every draw.
All inputs are finite; a program needn't handle non-finite values.
Results may differ from the reference program's by a relative error of at most 0.024.
Values may be sent and summed in bfloat16 or wider, within the bound.
No kernel may reach another device: no remote copies, remote signals or barrier semaphores. Data moves between devices by JAX's collectives and lax.ppermute only.
A program may use at most 320 MiB of HBM per device.

```python
import jax
import jax.numpy as jnp
from jax import lax

D = 768
HEADS = 12
HEAD = 64
FF = 3072
CLIPS_DEV = 4
SIDE_BASE = 10
SIDE_STEP = 4
SLOT = 324
VIEWS = 4
CLIPS = 32
TOKENS = 10368
N_DP = 8


def draw_item_class(key, part):
    key = jax.random.fold_in(key, 7)
    class_key, spot_key = jax.random.split(key)
    values = jax.random.randint(class_key, (CLIPS,), 0, 3, dtype=jnp.int32)
    spot = jax.random.randint(spot_key, (), 0, CLIPS, dtype=jnp.int32)
    values = values.at[spot].set(2)
    values = values.at[(spot + 1) % CLIPS].set(0)
    return values


def shard_levels(key, dims, cuts, smallest, high):
    loudness, own = 1.0, jax.random.fold_in(key, 6)
    for axis_at, parts in cuts:
        heights = jnp.exp(jax.random.uniform(jax.random.fold_in(own, axis_at), (parts,), jnp.float32, smallest / len(cuts), high / len(cuts)))
        loudness = loudness * jnp.repeat(heights, dims[axis_at] // parts).reshape([-1 if axis == axis_at else 1 for axis in range(len(dims))])
    return loudness


def gaussian(rng, dims, scale, most, cuts=(), kind=jnp.bfloat16):
    factor_of = shard_levels(rng, dims, cuts, -0.22, 0.18) if cuts else 1.0
    values = jax.random.normal(rng, dims, jnp.float32) * scale * factor_of
    return jnp.minimum(jnp.maximum(values, -most), most).astype(kind)


def setup_inputs(seed: int = 0) -> dict:
    key_list = jax.random.split(jax.random.key(seed), 13)
    tokens = gaussian(key_list[0], (VIEWS, TOKENS, D), 1.0, 6.0, ((0, 4), (1, 8)))
    item_class = draw_item_class(jax.random.fold_in(key_list[12], 71), 0)
    norm_gain = jnp.clip(1.0 + 0.1 * jax.random.normal(key_list[2], (VIEWS, 3, D), jnp.float32), 0.5, 1.5)
    norm_bias = gaussian(key_list[3], (VIEWS, 3, D), 0.3, 1.75, ((0, 4),), jnp.float32)
    attn_qkv = gaussian(key_list[4], (VIEWS, D, 3 * D), D ** -0.5, 0.21875, ((0, 4),))
    attn_out = gaussian(key_list[5], (VIEWS, D, D), (D // 16) ** -0.5, 0.875, ((0, 4),))
    mlp_up = gaussian(key_list[6], (VIEWS, D, FF), D ** -0.5, 0.21875, ((0, 4),))
    mlp_down = gaussian(key_list[7], (VIEWS, FF, D), FF ** -0.5, 0.109375, ((0, 4),))
    join_query = gaussian(key_list[8], (VIEWS, D, D), D ** -0.5, 0.21875, ((0, 4),))
    join_keyval = gaussian(key_list[9], (VIEWS, D, 2 * D), D ** -0.5, 0.21875, ((0, 4),))
    join_output = gaussian(key_list[10], (VIEWS, D, D), (D // 16) ** -0.5, 0.875, ((0, 4),))
    cotangent = gaussian(key_list[11], (VIEWS, TOKENS, D), 1.0, 6.0, ((0, 4), (1, 8)))
    return dict(tokens=tokens, item_class=item_class, norm_gain=norm_gain, norm_bias=norm_bias, attn_qkv=attn_qkv, attn_out=attn_out, mlp_up=mlp_up, mlp_down=mlp_down, join_query=join_query, join_keyval=join_keyval, join_output=join_output, cotangent=cotangent)


@jax.custom_vjp
def low(v):
    return lax.optimization_barrier(v.astype(jnp.bfloat16)).astype(jnp.float32)

@jax.custom_vjp
def low_back(v):
    return v

def low_keep(v):
    return (low(v), None)

def low_pass(kept, grad):
    return (grad,)

def back_keep(v):
    return (v, None)

def backward_reduced_precision(kept, grad):
    return (low(grad),)
low.defvjp(low_keep, low_pass)
low_back.defvjp(back_keep, backward_reduced_precision)

def norm_rows(values, gain_row, bias_row):
    centre = lax.optimization_barrier(jnp.mean(values, -1, keepdims=True))
    centred = values - centre
    spread = lax.optimization_barrier(jnp.mean(centred * centred, -1, keepdims=True))
    return centred * lax.rsqrt(spread + 1e-05) * gain_row + bias_row

def project(left_neighbour_view, right_neighbour_view):
    return jnp.dot(left_neighbour_view, right_neighbour_view, precision=lax.Precision.HIGHEST, preferred_element_type=jnp.float32)

def project_views(left_neighbour_view, right_neighbour_view):
    return jnp.einsum('nqj,njl->nql', left_neighbour_view, right_neighbour_view, precision=lax.Precision.HIGHEST)

def valid_slots(classes):
    sides = SIDE_BASE + SIDE_STEP * classes
    places = jnp.arange(SLOT, dtype=jnp.int32)
    return places[None, :] < (sides * sides)[:, None]

def attention(queries, key_rows, value_rows, valid):
    count = valid.shape[0]
    query_heads = queries.reshape(count, SLOT, HEADS, HEAD)
    key_heads = key_rows.reshape(count, SLOT, HEADS, HEAD)
    value_heads = value_rows.reshape(count, SLOT, HEADS, HEAD)
    scores = jnp.einsum('cqhd,ckhd->chqk', query_heads, key_heads, precision=lax.Precision.HIGHEST) * HEAD ** (-0.5)
    scores = low_back(scores)
    scores = jnp.where(valid[:, None, None, :], scores, -1e+30)
    largest = lax.optimization_barrier(jnp.max(scores, -1, keepdims=True))
    exp_scores = jnp.exp(scores - largest)
    probs = low(exp_scores / lax.optimization_barrier(jnp.sum(exp_scores, -1, keepdims=True)))
    mixed = jnp.einsum('chqk,ckhd->cqhd', probs, value_heads, precision=lax.Precision.HIGHEST)
    return mixed.reshape(count * SLOT, HEADS * HEAD)

def self_block(inputs, valid, gain_attn, bias_attn, gain_mlp, bias_mlp, weight_qkv, weight_out, weight_up, weight_down):
    width = inputs.shape[1]
    normed = low(norm_rows(inputs, gain_attn, bias_attn))
    triple = low(low_back(project(normed, weight_qkv)))
    mixed = attention(triple[:, :width], triple[:, width:2 * width], triple[:, 2 * width:], valid)
    branch = low_back(project(low(low_back(mixed)), weight_out))
    middle = inputs + branch
    normed_two = low(norm_rows(middle, gain_mlp, bias_mlp))
    hidden = low_back(project(normed_two, weight_up))
    activated = low(jax.nn.gelu(hidden))
    return middle + low_back(project(activated, weight_down))

def join_group(params, inputs, classes):
    norm_gain, norm_bias, attn_qkv, attn_out, mlp_up, mlp_down, join_query, join_keyval, join_output = params
    width = inputs.shape[2]
    valid = valid_slots(classes)
    live_rows = valid.reshape(-1).astype(jnp.float32)
    layer_one = jax.vmap(self_block, in_axes=(0, None, 0, 0, 0, 0, 0, 0, 0, 0))(inputs, valid, norm_gain[:, 0], norm_bias[:, 0], norm_gain[:, 1], norm_bias[:, 1], attn_qkv, attn_out, mlp_up, mlp_down)
    normed = low(norm_rows(layer_one, norm_gain[:, 2][:, None, :], norm_bias[:, 2][:, None, :]))
    join_queries = low(low_back(project_views(normed, join_query)))
    join_pairs = low(low_back(project_views(normed, join_keyval)))
    arrived = jnp.roll(join_pairs, -1, axis=0)
    mixed = jax.vmap(attention, in_axes=(0, 0, 0, None))(join_queries, arrived[:, :, :width], arrived[:, :, width:], valid)
    branch = low_back(project_views(low(low_back(mixed)), join_output))
    return (layer_one + branch) * live_rows[None, :, None]

def reference(tokens, item_class, norm_gain, norm_bias, attn_qkv, attn_out, mlp_up, mlp_down, join_query, join_keyval, join_output, cotangent):
    rows_dev = CLIPS_DEV * SLOT
    class_groups = item_class.reshape(N_DP, CLIPS_DEV)

    def forward(tokens_float, *params):
        blocks = tokens_float.reshape(VIEWS, N_DP, rows_dev, D).transpose(1, 0, 2, 3)

        def one_group(group_data):
            return join_group(params, group_data[0], group_data[1])
        outputs = lax.map(jax.checkpoint(one_group), (blocks, class_groups))
        return outputs.transpose(1, 0, 2, 3).reshape(VIEWS, TOKENS, D)
    floats = [tokens.astype(jnp.float32), norm_gain.astype(jnp.float32), norm_bias.astype(jnp.float32), attn_qkv.astype(jnp.float32), attn_out.astype(jnp.float32), mlp_up.astype(jnp.float32), mlp_down.astype(jnp.float32), join_query.astype(jnp.float32), join_keyval.astype(jnp.float32), join_output.astype(jnp.float32)]
    joined_out, reverse_mode_function = jax.vjp(forward, *floats)
    gradients = reverse_mode_function(cotangent.astype(jnp.float32))
    return (joined_out.astype(jnp.bfloat16), gradients[0], gradients[1], gradients[2], gradients[3], gradients[4], gradients[5], gradients[6], gradients[7], gradients[8], gradients[9])
```

```python
import functools

import jax
import jax.numpy as jnp
from jax import lax
from jax.experimental import pallas as pl
from jax.experimental.pallas import tpu as pltpu
from jax.sharding import PartitionSpec as P

HEADS = 12
HEAD = 64
SLOT = 324
CLASSES = ((112, 100), (208, 196), (336, 324))
MOST = 336
EPS = 1e-05
GELU_A = 0.7978845608028654
GELU_B = 0.044715
BF = jnp.bfloat16
F32 = jnp.float32


def dot(left, right, left_dim, right_dim):
    return lax.dot_general(
        left, right, (((left_dim,), (right_dim,)), ((), ())), preferred_element_type=F32
    )


def params(limit_mib=58):
    return pltpu.CompilerParams(vmem_limit_bytes=limit_mib * 2**20)


def cost(flops, moved):
    return pl.CostEstimate(flops=int(flops), bytes_accessed=int(moved), transcendentals=0)


def rows_of(item):
    return 112 + jnp.where(item >= 1, 96, 0) + jnp.where(item >= 2, 128, 0)


def start_of(cls_ref, clip):
    start = jnp.int32(0)
    for before in range(clip):
        start = start + rows_of(cls_ref[before])
    return pl.multiple_of(start, 16)


def start_dyn(cls_ref, clip, clips):
    start = jnp.int32(0)
    for before in range(clips):
        start = start + jnp.where(before < clip, rows_of(cls_ref[before]), 0)
    return pl.multiple_of(start, 16)


def total_of(cls_ref, clips):
    return start_of(cls_ref, clips)


def clear_tail(cls_ref, clips, refs):
    rows = refs[0].shape[0]
    total = total_of(cls_ref, clips)

    @pl.loop(0, (rows - total) // 16)
    def _(step):
        at = pl.ds(pl.multiple_of(total + step * 16, 16), 16)
        for ref in refs:
            ref[at, :] = jnp.zeros((16, ref.shape[1]), ref.dtype)


def by_class(item, body):
    for index, (rows, live) in enumerate(CLASSES):
        pl.when(item == index)(functools.partial(body, rows, live))


def norm_stats(values):
    centre = jnp.mean(values, -1, keepdims=True)
    centred = values - centre
    spread = jnp.mean(centred * centred, -1, keepdims=True)
    root = lax.rsqrt(spread + EPS)
    return centred * root, root


def norm_back(values, gain, grad, gain_acc, bias_acc):
    unit, root = norm_stats(values)
    gain_acc[...] += jnp.sum(grad * unit, 0, keepdims=True)
    bias_acc[...] += jnp.sum(grad, 0, keepdims=True)
    scaled = grad * gain
    return root * (
        scaled
        - jnp.mean(scaled, -1, keepdims=True)
        - unit * jnp.mean(scaled * unit, -1, keepdims=True)
    )


def interleave(stages, count):
    held = [dict() for _ in range(count)]
    for step in range(count + len(stages) - 1):
        for index, stage in enumerate(stages):
            if 0 <= step - index < count:
                stage(step - index, held[step - index])


def one_head(pair, head):
    lane = lax.broadcasted_iota(jnp.int32, pair.shape, 1)
    keep = lane < HEAD if head % 2 == 0 else lane >= HEAD
    return jnp.where(keep, pair, jnp.zeros_like(pair))


def pair_of(head):
    return slice(128 * (head // 2), 128 * (head // 2) + 128)


def mask_keys_lane(scores, live):
    lane = lax.broadcasted_iota(jnp.int32, scores.shape, 1)
    return jnp.where(lane < live, scores, -1e30)


def mask_keys_row(scores, live):
    head, tail = scores[:-16], scores[-16:]
    row = lax.broadcasted_iota(jnp.int32, tail.shape, 0)
    tail = jnp.where(row < live - head.shape[0], tail, -1e30)
    return jnp.concatenate([head, tail], axis=0)


def attend(load_q, load_k, load_v, store, live):
    pairs = {}

    def score(head, held):
        query = one_head(load_q(head), head) * jnp.asarray(HEAD**-0.5, BF)
        held["s"] = mask_keys_lane(dot(query, load_k(head), 1, 1), live)

    def soften(head, held):
        scores = held.pop("s")
        exps = jnp.exp(scores - jnp.max(scores, -1, keepdims=True))
        held["l"] = jnp.sum(exps, -1, keepdims=True)
        held["e"] = exps.astype(BF)

    def mix(head, held):
        mixed = dot(held.pop("e"), one_head(load_v(head), head), 1, 0) / held.pop("l")
        if head % 2 == 0:
            pairs[head // 2] = mixed
        else:
            store(head, (pairs.pop(head // 2) + mixed).astype(BF))

    interleave([score, soften, mix], HEADS)


def attend_back(load_q, load_k, load_v, load_do, load_o, store, live):
    cache = {}

    def turned(head, name, load, wide=False):
        key = (name, head // 2)
        if key not in cache:
            value = load(head).T
            cache[key] = value.astype(F32) if wide else value
        at = HEAD * (head % 2)
        return cache[key][at : at + HEAD]

    def score(head, held):
        held["q"] = one_head(load_q(head), head) * jnp.asarray(HEAD**-0.5, BF)
        held["s"] = mask_keys_row(dot(load_k(head), held["q"], 1, 1), live)
        held["do"] = one_head(load_do(head), head)
        held["dp"] = dot(load_v(head), held["do"], 1, 1)

    def soften(head, held):
        scores = held.pop("s")
        exps = jnp.exp(scores - jnp.max(scores, 0, keepdims=True))
        held["p"] = exps * (1.0 / jnp.sum(exps, 0, keepdims=True))
        held["pb"] = held["p"].astype(BF)

    def mix(head, held):
        if load_o is None:
            held["o"] = dot(turned(head, "v", load_v), held["pb"], 1, 0)
        else:
            held["o"] = turned(head, "o", load_o, True)

    def grad_score(head, held):
        row_terms = jnp.sum(held["o"] * turned(head, "do", load_do, True), 0, keepdims=True)
        held["ds"] = (held.pop("p") * (held.pop("dp") - row_terms)).astype(BF)

    def finish(head, held):
        grad = held.pop("ds")
        held["dv"] = dot(held.pop("pb"), held.pop("do"), 1, 0)
        held["dk"] = dot(grad, held.pop("q"), 1, 0)
        held["dq"] = dot(turned(head, "k", load_k), grad, 1, 0) * HEAD**-0.5
        if head % 2 == 0:
            cache["half"] = held
            return
        first = cache.pop("half")
        mixed = None
        if load_o is None:
            mixed = jnp.concatenate([first["o"], held["o"]], 0).astype(BF).T
        query = jnp.concatenate([first["dq"], held["dq"]], 0).astype(BF).T
        store(
            head,
            query,
            (first["dk"] + held["dk"]).astype(BF),
            (first["dv"] + held["dv"]).astype(BF),
            mixed,
        )

    interleave([score, soften, mix, grad_score, finish], HEADS)


def pack_clip(cls_ref, clip, source, target, masked):
    start = start_of(cls_ref, clip)

    def copy(rows, live):
        held = min(rows, SLOT)
        value = source[clip * SLOT : clip * SLOT + held, :]
        if masked:
            row = lax.broadcasted_iota(jnp.int32, value.shape, 0)
            value = jnp.where(row < live, value, jnp.zeros_like(value))
        if rows > held:
            pad = jnp.zeros((rows - held, value.shape[1]), value.dtype)
            value = jnp.concatenate([value, pad], 0)
        target[pl.ds(start, rows), :] = value

    by_class(cls_ref[clip], copy)


def whole(shape):
    zeros = (0,) * len(shape)
    return pl.BlockSpec(shape, lambda *_: zeros, pipeline_mode=pl.Buffered(1))


def whole_out(shape):
    zeros = (0,) * len(shape)
    return pl.BlockSpec(shape, lambda *_: zeros)


def tile(rows, columns):
    return pl.BlockSpec((rows, columns), lambda i, *_: (i, 0))


def pack_rows(cotangent, classes, rows):
    clips = classes.shape[0]
    width = cotangent.shape[1]

    def kernel(cls_ref, source, target):
        for clip in range(clips):
            pack_clip(cls_ref, clip, source, target, True)
        clear_tail(cls_ref, clips, [target])

    return pl.pallas_call(
        kernel,
        grid_spec=pltpu.PrefetchScalarGridSpec(
            num_scalar_prefetch=1,
            grid=(1,),
            in_specs=[whole(cotangent.shape)],
            out_specs=whole_out((rows, width)),
        ),
        out_shape=jax.ShapeDtypeStruct((rows, width), BF),
        compiler_params=params(),
        cost_estimate=cost(0, 4 * rows * width),
    )(classes, cotangent)


def norm_project(tokens, classes, rows, gain, bias, weight, step):
    clips = classes.shape[0]
    width, wide = weight.shape

    def kernel(cls_ref, tok_ref, gain_ref, bias_ref, w_ref, x_ref, h_ref, qkv_ref):
        index = pl.program_id(0)

        @pl.when(index == 0)
        def _():
            for clip in range(clips):
                pack_clip(cls_ref, clip, tok_ref, x_ref, False)
            clear_tail(cls_ref, clips, [x_ref])

        live = index * step < total_of(cls_ref, clips)

        @pl.when(live)
        def _():
            at = pl.ds(pl.multiple_of(index * step, 16), step)
            unit, _ = norm_stats(x_ref[at, :].astype(F32))
            low = (unit * gain_ref[...] + bias_ref[...]).astype(BF)
            h_ref[...] = low
            qkv_ref[...] = dot(low, w_ref[...], 1, 0).astype(BF)

        @pl.when(jnp.logical_not(live))
        def _():
            h_ref[...] = jnp.zeros_like(h_ref)
            qkv_ref[...] = jnp.zeros_like(qkv_ref)

    return pl.pallas_call(
        kernel,
        grid_spec=pltpu.PrefetchScalarGridSpec(
            num_scalar_prefetch=1,
            grid=(rows // step,),
            in_specs=[whole(tokens.shape), whole(gain.shape), whole(bias.shape), whole(weight.shape)],
            out_specs=[whole_out((rows, width)), tile(step, width), tile(step, wide)],
        ),
        out_shape=[
            jax.ShapeDtypeStruct((rows, width), BF),
            jax.ShapeDtypeStruct((rows, width), BF),
            jax.ShapeDtypeStruct((rows, wide), BF),
        ],
        compiler_params=params(),
        cost_estimate=cost(2 * rows * width * wide, 2 * rows * (3 * width + wide) + 2 * weight.size),
    )(classes, tokens, gain, bias, weight)


def self_attend(qkv, classes):
    clips = classes.shape[0]
    rows, wide = qkv.shape
    width = wide // 3

    def kernel(cls_ref, qkv_ref, o_ref):
        clip = pl.program_id(0)
        start = start_dyn(cls_ref, clip, clips)

        def body(count, live):
            at = pl.ds(start, count)

            def load(part):
                def get(head):
                    pair = pair_of(head)
                    return qkv_ref[at, part * width + pair.start : part * width + pair.stop]

                return get

            def store(head, mixed):
                o_ref[at, pair_of(head)] = mixed

            attend(load(0), load(1), load(2), store, live)

        by_class(cls_ref[clip], body)

        @pl.when(clip == clips - 1)
        def _():
            clear_tail(cls_ref, clips, [o_ref])

    return pl.pallas_call(
        kernel,
        grid_spec=pltpu.PrefetchScalarGridSpec(
            num_scalar_prefetch=1,
            grid=(clips,),
            in_specs=[whole(qkv.shape)],
            out_specs=whole_out((rows, width)),
        ),
        out_shape=jax.ShapeDtypeStruct((rows, width), BF),
        compiler_params=params(),
        cost_estimate=cost(16 * rows * MOST * width, 2 * rows * (wide + width)),
    )(classes, qkv)


def feed_forward(x, mixed, classes, gains, biases, w_out, w_up, w_down, w_fq, step):
    clips = classes.shape[0]
    rows, width = x.shape
    hidden = w_up.shape[1]
    chunk = width

    def kernel(
        cls_ref, x_ref, o_ref, gain_ref, bias_ref, out_w, up_w, down_w, fq_w,
        mid_ref, h_ref, u_ref, act_ref, layer_ref, n_ref, fq_ref,
    ):
        live = pl.program_id(0) * step < total_of(cls_ref, clips)

        @pl.when(live)
        def _():
            middle = x_ref[...].astype(F32) + dot(o_ref[...], out_w[...], 1, 0)
            mid_ref[...] = middle
            unit, _ = norm_stats(middle)
            low = (unit * gain_ref[1:2] + bias_ref[1:2]).astype(BF)
            h_ref[...] = low
            layer = middle
            for at in range(0, hidden, chunk):
                part = slice(at, at + chunk)
                up = dot(low, up_w[:, part], 1, 0)
                inner = jnp.tanh(GELU_A * (up + GELU_B * (up * up * up)))
                act = (0.5 * up * (1.0 + inner)).astype(BF)
                u_ref[:, part] = up.astype(BF)
                act_ref[:, part] = act
                layer = layer + dot(act, down_w[part, :], 1, 0)
            layer_ref[...] = layer
            unit, _ = norm_stats(layer)
            low = (unit * gain_ref[2:3] + bias_ref[2:3]).astype(BF)
            n_ref[...] = low
            fq_ref[...] = dot(low, fq_w[...], 1, 0).astype(BF)

        @pl.when(jnp.logical_not(live))
        def _():
            for ref in (mid_ref, h_ref, u_ref, act_ref, layer_ref, n_ref, fq_ref):
                ref[...] = jnp.zeros_like(ref)

    shapes = [(width, F32), (width, BF), (hidden, BF), (hidden, BF), (width, F32), (width, BF), (width, BF)]
    weights = [w_out, w_up, w_down, w_fq]
    return pl.pallas_call(
        kernel,
        grid_spec=pltpu.PrefetchScalarGridSpec(
            num_scalar_prefetch=1,
            grid=(rows // step,),
            in_specs=[tile(step, width), tile(step, width), whole(gains.shape), whole(biases.shape)]
            + [whole(w.shape) for w in weights],
            out_specs=[tile(step, columns) for columns, _ in shapes],
        ),
        out_shape=[jax.ShapeDtypeStruct((rows, columns), kind) for columns, kind in shapes],
        compiler_params=params(),
        cost_estimate=cost(
            2 * rows * sum(w.size for w in weights),
            2 * sum(w.size for w in weights) + rows * (4 * 5 * width + 4 * hidden),
        ),
    )(classes, x, mixed, gains, biases, *weights)


def join_attend(arrived, fq, grad, w_kv, w_out, classes):
    clips = classes.shape[0]
    rows, width = fq.shape
    wide = w_kv.shape[1]

    def kernel(cls_ref, n_ref, q_ref, g_ref, kv_w, out_w, o_ref, dq_ref, dkv_ref, dn_ref, kv, do):
        clip = pl.program_id(0)
        start = start_dyn(cls_ref, clip, clips)

        def body(count, live):
            at = pl.ds(start, count)
            kv[:count, :] = dot(n_ref[at, :], kv_w[...], 1, 0).astype(BF)
            do[:count, :] = dot(g_ref[at, :], out_w[...], 1, 1).astype(BF)

            def load_q(head):
                return q_ref[at, pair_of(head)]

            def load_k(head):
                return kv[:count, pair_of(head)]

            def load_v(head):
                pair = pair_of(head)
                return kv[:count, width + pair.start : width + pair.stop]

            def load_do(head):
                return do[:count, pair_of(head)]

            def store(head, query, key, value, mixed):
                pair = pair_of(head)
                o_ref[at, pair] = mixed
                dq_ref[at, pair] = query
                dkv_ref[at, pair] = key
                dkv_ref[at, width + pair.start : width + pair.stop] = value

            attend_back(load_q, load_k, load_v, load_do, None, store, live)
            dn_ref[at, :] = dot(dkv_ref[at, :], kv_w[...], 1, 1).astype(BF)

        by_class(cls_ref[clip], body)

        @pl.when(clip == clips - 1)
        def _():
            clear_tail(cls_ref, clips, [o_ref, dq_ref, dkv_ref, dn_ref])

    outs = [width, width, wide, width]
    return pl.pallas_call(
        kernel,
        grid_spec=pltpu.PrefetchScalarGridSpec(
            num_scalar_prefetch=1,
            grid=(clips,),
            in_specs=[whole(v.shape) for v in (arrived, fq, grad, w_kv, w_out)],
            out_specs=[whole_out((rows, columns)) for columns in outs],
            scratch_shapes=[pltpu.VMEM((MOST, wide), BF), pltpu.VMEM((MOST, width), BF)],
        ),
        out_shape=[jax.ShapeDtypeStruct((rows, columns), BF) for columns in outs],
        compiler_params=params(),
        cost_estimate=cost(64 * rows * MOST * width, 20 * rows * width),
    )(classes, arrived, fq, grad, w_kv, w_out)


def join_result(layer, mixed, w_out, classes, slots):
    clips = classes.shape[0]
    rows, width = layer.shape

    def kernel(cls_ref, layer_ref, o_ref, w_ref, out_ref):
        for clip in range(clips):
            start = start_of(cls_ref, clip)

            def body(count, live):
                at = pl.ds(start, count)
                value = layer_ref[at, :] + dot(o_ref[at, :], w_ref[...], 1, 0)
                held = min(count, SLOT)
                row = lax.broadcasted_iota(jnp.int32, value.shape, 0)
                value = jnp.where(row < live, value, 0.0).astype(BF)
                first = clip * SLOT
                out_ref[first : first + held, :] = value[:held]
                if held < SLOT:
                    out_ref[first + held : first + SLOT, :] = jnp.zeros((SLOT - held, width), BF)

            by_class(cls_ref[clip], body)

    return pl.pallas_call(
        kernel,
        grid_spec=pltpu.PrefetchScalarGridSpec(
            num_scalar_prefetch=1,
            grid=(1,),
            in_specs=[whole(v.shape) for v in (layer, mixed, w_out)],
            out_specs=whole_out((slots, width)),
        ),
        out_shape=jax.ShapeDtypeStruct((slots, width), BF),
        compiler_params=params(),
        cost_estimate=cost(2 * rows * width * width, 8 * rows * width + 2 * w_out.size),
    )(classes, layer, mixed, w_out)


def feed_forward_back(dfq, back, layer, grad, up, middle, classes, gains, w_fq, w_down, w_up, w_out, step):
    clips = classes.shape[0]
    rows, width = layer.shape
    hidden = w_up.shape[1]
    chunk = width

    def kernel(
        cls_ref, dfq_ref, back_ref, layer_ref, g_ref, u_ref, mid_ref, gain_ref, fq_w, down_w, up_w, out_w,
        down_ref, hid_ref, gmid_ref, low_ref, do_ref, gain_three, bias_three, gain_two, bias_two,
    ):
        @pl.when(pl.program_id(0) == 0)
        def _():
            for ref in (gain_three, bias_three, gain_two, bias_two):
                ref[...] = jnp.zeros_like(ref)

        live = pl.program_id(0) * step < total_of(cls_ref, clips)

        @pl.when(live)
        def _():
            grad_norm = dot(dfq_ref[...], fq_w[...], 1, 1) + back_ref[...].astype(F32)
            grad_layer = g_ref[...].astype(F32) + norm_back(
                layer_ref[...], gain_ref[2:3], grad_norm, gain_three, bias_three
            )
            down_low = grad_layer.astype(BF)
            down_ref[...] = down_low
            grad_norm = jnp.zeros((step, width), F32)
            for at in range(0, hidden, chunk):
                part = slice(at, at + chunk)
                grad_act = dot(down_low, down_w[part, :], 1, 1)
                value = u_ref[:, part].astype(F32)
                square = value * value
                inner = jnp.tanh(GELU_A * (value + GELU_B * (square * value)))
                slope = 0.5 * (1.0 + inner) + (0.5 * GELU_A) * value * (1.0 - inner * inner) * (
                    1.0 + (3.0 * GELU_B) * square
                )
                low = (grad_act * slope).astype(BF)
                hid_ref[:, part] = low
                grad_norm = grad_norm + dot(low, up_w[:, part], 1, 1)
            grad_middle = grad_layer + norm_back(
                mid_ref[...], gain_ref[1:2], grad_norm, gain_two, bias_two
            )
            gmid_ref[...] = grad_middle
            low = grad_middle.astype(BF)
            low_ref[...] = low
            do_ref[...] = dot(low, out_w[...], 1, 1).astype(BF)

        @pl.when(jnp.logical_not(live))
        def _():
            for ref in (down_ref, hid_ref, gmid_ref, low_ref, do_ref):
                ref[...] = jnp.zeros_like(ref)

    shapes = [(width, BF), (hidden, BF), (width, F32), (width, BF), (width, BF)]
    weights = [w_fq, w_down, w_up, w_out]
    return pl.pallas_call(
        kernel,
        grid_spec=pltpu.PrefetchScalarGridSpec(
            num_scalar_prefetch=1,
            grid=(rows // step,),
            in_specs=[
                tile(step, width), tile(step, width), tile(step, width), tile(step, width),
                tile(step, hidden), tile(step, width), whole(gains.shape),
            ]
            + [whole(w.shape) for w in weights],
            out_specs=[tile(step, columns) for columns, _ in shapes] + [whole_out((1, width))] * 4,
        ),
        out_shape=[jax.ShapeDtypeStruct((rows, columns), kind) for columns, kind in shapes]
        + [jax.ShapeDtypeStruct((1, width), F32)] * 4,
        compiler_params=params(),
        cost_estimate=cost(
            2 * rows * sum(w.size for w in weights),
            2 * sum(w.size for w in weights) + rows * (4 * 7 * width + 4 * hidden),
        ),
    )(classes, dfq, back, layer, grad, up, middle, gains, *weights)


def self_attend_back(qkv, mixed, grad, classes):
    clips = classes.shape[0]
    rows, wide = qkv.shape
    width = wide // 3

    def kernel(cls_ref, qkv_ref, o_ref, do_ref, d_ref):
        clip = pl.program_id(0)
        start = start_dyn(cls_ref, clip, clips)

        def body(count, live):
            at = pl.ds(start, count)

            def columns(part, head):
                pair = pair_of(head)
                return slice(part * width + pair.start, part * width + pair.stop)

            def load(part):
                return lambda head: qkv_ref[at, columns(part, head)]

            def store(head, query, key, value, _):
                for part, result in enumerate((query, key, value)):
                    d_ref[at, columns(part, head)] = result

            attend_back(
                load(0),
                load(1),
                load(2),
                lambda head: do_ref[at, pair_of(head)],
                lambda head: o_ref[at, pair_of(head)],
                store,
                live,
            )

        by_class(cls_ref[clip], body)

        @pl.when(clip == clips - 1)
        def _():
            clear_tail(cls_ref, clips, [d_ref])

    return pl.pallas_call(
        kernel,
        grid_spec=pltpu.PrefetchScalarGridSpec(
            num_scalar_prefetch=1,
            grid=(clips,),
            in_specs=[whole(v.shape) for v in (qkv, mixed, grad)],
            out_specs=whole_out((rows, wide)),
        ),
        out_shape=jax.ShapeDtypeStruct((rows, wide), BF),
        compiler_params=params(),
        cost_estimate=cost(48 * rows * MOST * width, 16 * rows * width),
    )(classes, qkv, mixed, grad)


def norm_project_back(dqkv, x, gmid, classes, gain, weight, step, slots):
    clips = classes.shape[0]
    rows, width = x.shape
    wide = weight.shape[1]

    def kernel(cls_ref, d_ref, x_ref, gmid_ref, gain_ref, w_ref, out_ref, gain_one, bias_one, packed):
        index = pl.program_id(0)

        @pl.when(index == 0)
        def _():
            gain_one[...] = jnp.zeros_like(gain_one)
            bias_one[...] = jnp.zeros_like(bias_one)

        @pl.when(index * step < total_of(cls_ref, clips))
        def _():
            grad_norm = dot(d_ref[...], w_ref[...], 1, 1)
            at = pl.ds(pl.multiple_of(index * step, 16), step)
            packed[at, :] = gmid_ref[...] + norm_back(
                x_ref[...].astype(F32), gain_ref[...], grad_norm, gain_one, bias_one
            )

        @pl.when(index == rows // step - 1)
        def _():
            for clip in range(clips):
                start = start_of(cls_ref, clip)

                def body(count, live):
                    value = packed[pl.ds(start, count), :]
                    held = min(count, SLOT)
                    first = clip * SLOT
                    out_ref[first : first + held, :] = value[:held]
                    if held < SLOT:
                        out_ref[first + held : first + SLOT, :] = jnp.zeros((SLOT - held, width), F32)

                by_class(cls_ref[clip], body)

    return pl.pallas_call(
        kernel,
        grid_spec=pltpu.PrefetchScalarGridSpec(
            num_scalar_prefetch=1,
            grid=(rows // step,),
            in_specs=[
                tile(step, wide), tile(step, width), tile(step, width), whole(gain.shape), whole(weight.shape),
            ],
            out_specs=[whole_out((slots, width))] + [whole_out((1, width))] * 2,
            scratch_shapes=[pltpu.VMEM((rows, width), F32)],
        ),
        out_shape=[jax.ShapeDtypeStruct((slots, width), F32)] + [jax.ShapeDtypeStruct((1, width), F32)] * 2,
        compiler_params=params(),
        cost_estimate=cost(2 * rows * width * wide, rows * (10 * width + 2 * wide) + 2 * weight.size),
    )(classes, dqkv, x, gmid, gain, weight)


def bits_of(count):
    return count.bit_length() - 1


def place_to_part(place, order):
    part = 0
    for index, bit in enumerate(order):
        if place >> (len(order) - 1 - index) & 1:
            part |= 1 << bit
    return part


def weight_grads(own, products, shards, order):
    width = products[0][0].shape[1]
    rows = products[0][0].shape[0]
    blocks = [right.shape[1] // width for _, right in products]
    total = sum(blocks)
    part_rows = width // shards
    half = shards // 2

    def kernel(own_ref, *refs):
        lefts = refs[: len(products)]
        rights = refs[len(products) : 2 * len(products)]
        kept, sent, acc = refs[2 * len(products) :]
        index = pl.program_id(0)
        first = 0
        for left, right, count in zip(lefts, rights, blocks):

            @pl.when((index >= first) & (index < first + count))
            def _():
                acc[...] = dot(left[...], right[...], 0, 0)

            first += count
        for place in range(shards):
            owner = own_ref[0] ^ place_to_part(place, order)
            part = acc[pl.ds(pl.multiple_of(owner * part_rows, 8), part_rows), :].astype(BF)
            if place < half:
                kept[place] = part
            else:
                sent[place - half] = part

    def right_spec(first, count):
        return pl.BlockSpec((rows, width), lambda j, *_: (0, jnp.clip(j - first, 0, count - 1)))

    firsts = [sum(blocks[:i]) for i in range(len(blocks))]
    out = pl.BlockSpec((half, part_rows, width), lambda j, *_: (0, 0, j))
    return pl.pallas_call(
        kernel,
        grid_spec=pltpu.PrefetchScalarGridSpec(
            num_scalar_prefetch=1,
            grid=(total,),
            in_specs=[whole(left.shape) for left, _ in products]
            + [right_spec(first, count) for first, count in zip(firsts, blocks)],
            out_specs=[out, out],
            scratch_shapes=[pltpu.VMEM((width, width), F32)],
        ),
        out_shape=[jax.ShapeDtypeStruct((half, part_rows, width * total), BF)] * 2,
        compiler_params=params(),
        cost_estimate=cost(
            2 * rows * width * width * total,
            2 * rows * width * (len(products) + total) + 2 * width * width * total,
        ),
    )(own, *[left for left, _ in products], *[right for _, right in products])


def weight_grads_tall(own, left, right, shards, order):
    rows, tall = left.shape
    width = right.shape[1]
    part_rows = tall // shards
    half = shards // 2
    blocks = tall // width
    per_block = width // part_rows

    def kernel(own_ref, left_ref, right_ref, kept, sent, acc):
        index = pl.program_id(0)
        acc[...] = dot(left_ref[...], right_ref[...], 0, 0)
        for sub in range(per_block):
            part = acc[sub * part_rows : (sub + 1) * part_rows, :].astype(BF)
            distance = own_ref[0] ^ (index * per_block + sub)
            place = jnp.int32(0)
            for position, bit in enumerate(order):
                place = place | (((distance >> bit) & 1) << (len(order) - 1 - position))

            @pl.when(place < half)
            def _():
                kept[jnp.minimum(place, half - 1)] = part

            @pl.when(place >= half)
            def _():
                sent[jnp.maximum(place - half, 0)] = part

    return pl.pallas_call(
        kernel,
        grid_spec=pltpu.PrefetchScalarGridSpec(
            num_scalar_prefetch=1,
            grid=(blocks,),
            in_specs=[pl.BlockSpec((rows, width), lambda j, *_: (0, j)), whole(right.shape)],
            out_specs=[whole_out((half, part_rows, width))] * 2,
            scratch_shapes=[pltpu.VMEM((width, width), F32)],
        ),
        out_shape=[jax.ShapeDtypeStruct((half, part_rows, width), BF)] * 2,
        compiler_params=params(),
        cost_estimate=cost(2 * rows * tall * width, 2 * rows * (tall + width) + 2 * tall * width),
    )(own, left, right)


def exchange(value, bit):
    count = lax.axis_size("dp")
    return lax.ppermute(value, "dp", [(i, i ^ (1 << bit)) for i in range(count)])


def halve(kept, sent, order):
    for index, bit in enumerate(order):
        got = exchange(sent, bit)
        value = kept.astype(F32) + got.astype(F32)
        if index == len(order) - 1:
            return value[0]
        low = value.astype(BF)
        half = low.shape[0] // 2
        kept, sent = low[:half], low[half:]


def shifted(value, axis, steps):
    count = lax.axis_size(axis)
    return lax.ppermute(value, axis, [(source, (source + steps) % count) for source in range(count)])


def per_device(
    tokens, item_class, norm_gain, norm_bias, attn_qkv, attn_out, mlp_up, mlp_down,
    join_query, join_keyval, join_output, cotangent,
):
    width = tokens.shape[2]
    slots = tokens.shape[1]
    clips = item_class.shape[0]
    rows = clips * MOST
    shards = lax.axis_size("dp")
    step = MOST
    gains, biases = norm_gain[0], norm_bias[0]
    w_qkv, w_out, w_up, w_down = attn_qkv[0], attn_out[0], mlp_up[0], mlp_down[0]
    w_fq, w_fkv, w_fo = join_query[0], join_keyval[0], join_output[0]
    own = lax.axis_index("dp").astype(jnp.int32)[None]

    next_fkv = shifted(w_fkv, "view", -1)
    x, low_one, qkv = norm_project(tokens[0], item_class, rows, gains[:1], biases[:1], w_qkv, step)
    mixed = self_attend(qkv, item_class)
    middle, low_two, up, act, layer, low_three, fq = feed_forward(
        x, mixed, item_class, gains, biases, w_out, w_up, w_down, w_fq, step
    )
    arrived = shifted(low_three, "view", -1)
    grad = pack_rows(cotangent[0], item_class, rows)
    join_mixed, dfq, dkv, back = join_attend(arrived, fq, grad, next_fkv, w_fo, item_class)
    returned = shifted(back, "view", 1)
    joined = join_result(layer, join_mixed, w_fo, item_class, slots)

    order = (0, 1, 2)
    sum_join = halve(
        *weight_grads(own, [(join_mixed, grad), (low_three, dfq), (arrived, dkv)], shards, order), order
    )
    down_low, hidden_low, gmid, out_low, do_self, gain_three, bias_three, gain_two, bias_two = feed_forward_back(
        dfq, returned, layer, grad, up, middle, item_class, gains, w_fq, w_down, w_up, w_out, step
    )
    sum_down = halve(*weight_grads_tall(own, act, down_low, shards, order), order)
    sum_up = halve(*weight_grads(own, [(low_two, hidden_low)], shards, order), order)
    dqkv = self_attend_back(qkv, mixed, do_self, item_class)
    sum_self = halve(*weight_grads(own, [(mixed, out_low), (low_one, dqkv)], shards, order), order)
    grad_tokens, gain_one, bias_one = norm_project_back(
        dqkv, x, gmid, item_class, gains[:1], w_qkv, step, slots
    )
    small = jnp.concatenate([gain_one, gain_two, gain_three, bias_one, bias_two, bias_three], 0)
    small = lax.psum_scatter(small, "dp", scatter_dimension=1, tiled=True)
    sum_fkv = shifted(sum_join[:, 2 * width :], "view", 1)
    return (
        joined[None],
        grad_tokens[None],
        small[None, :3],
        small[None, 3:],
        sum_self[None, :, width:],
        sum_self[None, :, :width],
        sum_up[None],
        sum_down[None],
        sum_join[None, :, width : 2 * width],
        sum_fkv[None],
        sum_join[None, :, :width],
    )


def solution(mesh):
    weight = P("view", None, None)
    tokens = P("view", "dp", None)
    small = P("view", None, "dp")
    return jax.shard_map(
        per_device,
        mesh=mesh,
        in_specs=(tokens, P("dp")) + (weight,) * 9 + (tokens,),
        out_specs=(tokens, tokens, small, small) + (tokens,) * 7,
        check_vma=False,
    )
```

```python
import functools

import jax
import jax.numpy as jnp
from jax import lax
from jax.experimental import pallas as pl
from jax.experimental.pallas import tpu as pltpu
from jax.sharding import PartitionSpec as P

HEADS = 12
HEAD = 64
SLOT = 324
CLASSES = ((112, 100), (208, 196), (336, 324))
MOST = 336
EPS = 1e-05
GELU_A = 0.7978845608028654
GELU_B = 0.044715
BF = jnp.bfloat16
F32 = jnp.float32


def dot(left, right, left_dim, right_dim):
    return lax.dot_general(
        left, right, (((left_dim,), (right_dim,)), ((), ())), preferred_element_type=F32
    )


def params(limit_mib=20):
    return pltpu.CompilerParams(vmem_limit_bytes=limit_mib * 2**20)


def cost(flops, moved):
    return pl.CostEstimate(flops=int(flops) // 2000, bytes_accessed=int(moved) // 2000, transcendentals=0)


def rows_of(item):
    return 112 + jnp.where(item >= 1, 96, 0) + jnp.where(item >= 2, 128, 0)


def start_of(cls_ref, clip):
    start = jnp.int32(0)
    for before in range(clip):
        start = start + rows_of(cls_ref[before])
    return pl.multiple_of(start, 16)


def start_dyn(cls_ref, clip, clips):
    start = jnp.int32(0)
    for before in range(clips):
        start = start + jnp.where(before < clip, rows_of(cls_ref[before]), 0)
    return pl.multiple_of(start, 16)


def total_of(cls_ref, clips):
    return start_of(cls_ref, clips)


def clear_from(total, refs):
    rows = refs[0].shape[0]

    @pl.loop(0, (rows - total) // 16)
    def _(step):
        at = pl.ds(pl.multiple_of(total + step * 16, 16), 16)
        for ref in refs:
            ref[at, :] = jnp.zeros((16, ref.shape[1]), ref.dtype)


def clear_tail(cls_ref, clips, refs):
    clear_from(total_of(cls_ref, clips), refs)


def merge(first, second, base, target):
    half = first.shape[0]
    target[:half, :] = first[...]
    target[half:, :] = jnp.zeros((target.shape[0] - half, target.shape[1]), target.dtype)
    target[pl.ds(base, half), :] = second[...]


def by_class(item, body):
    for index, (rows, live) in enumerate(CLASSES):
        pl.when(item == index)(functools.partial(body, rows, live))


def norm_stats(values):
    centre = jnp.mean(values, -1, keepdims=True)
    centred = values - centre
    spread = jnp.mean(centred * centred, -1, keepdims=True)
    root = lax.rsqrt(spread + EPS)
    return centred * root, root


def norm_back(values, gain, grad, gain_acc, bias_acc):
    unit, root = norm_stats(values)
    gain_acc[...] += jnp.sum(grad * unit, 0, keepdims=True)
    bias_acc[...] += jnp.sum(grad, 0, keepdims=True)
    scaled = grad * gain
    return root * (
        scaled
        - jnp.mean(scaled, -1, keepdims=True)
        - unit * jnp.mean(scaled * unit, -1, keepdims=True)
    )


def interleave(stages, count):
    held = [dict() for _ in range(count)]
    for step in range(count + len(stages) - 1):
        for index, stage in enumerate(stages):
            if 0 <= step - index < count:
                stage(step - index, held[step - index])


def one_head(pair, head):
    lane = lax.broadcasted_iota(jnp.int32, pair.shape, 1)
    keep = lane < HEAD if head % 2 == 0 else lane >= HEAD
    return jnp.where(keep, pair, jnp.zeros_like(pair))


def pair_of(head):
    return slice(128 * (head // 2), 128 * (head // 2) + 128)


def mask_keys_lane(scores, live):
    lane = lax.broadcasted_iota(jnp.int32, scores.shape, 1)
    return jnp.where(lane < live, scores, -1e30)


def mask_keys_row(scores, live):
    head, tail = scores[:-16], scores[-16:]
    row = lax.broadcasted_iota(jnp.int32, tail.shape, 0)
    tail = jnp.where(row < live - head.shape[0], tail, -1e30)
    return jnp.concatenate([head, tail], axis=0)


def attend(load_q, load_k, load_v, store, live):
    pairs = {}

    def score(head, held):
        query = one_head(load_q(head), head) * jnp.asarray(HEAD**-0.5, BF)
        held["s"] = mask_keys_lane(dot(query, load_k(head), 1, 1), live)

    def soften(head, held):
        scores = held.pop("s")
        exps = jnp.exp(scores - jnp.max(scores, -1, keepdims=True))
        held["l"] = jnp.sum(exps, -1, keepdims=True)
        held["e"] = exps.astype(BF)

    def mix(head, held):
        mixed = dot(held.pop("e"), one_head(load_v(head), head), 1, 0) / held.pop("l")
        if head % 2 == 0:
            pairs[head // 2] = mixed
        else:
            store(head, (pairs.pop(head // 2) + mixed).astype(BF))

    interleave([score, soften, mix], HEADS)


def attend_back(load_q, load_k, load_v, load_do, load_o, store, live):
    cache = {}

    def turned(head, name, load, wide=False):
        key = (name, head // 2)
        if key not in cache:
            value = load(head).T
            cache[key] = value.astype(F32) if wide else value
        at = HEAD * (head % 2)
        return cache[key][at : at + HEAD]

    def score(head, held):
        held["q"] = one_head(load_q(head), head) * jnp.asarray(HEAD**-0.5, BF)
        held["s"] = mask_keys_row(dot(load_k(head), held["q"], 1, 1), live)
        held["do"] = one_head(load_do(head), head)
        held["dp"] = dot(load_v(head), held["do"], 1, 1)

    def soften(head, held):
        scores = held.pop("s")
        exps = jnp.exp(scores - jnp.max(scores, 0, keepdims=True))
        held["p"] = exps * (1.0 / jnp.sum(exps, 0, keepdims=True))
        held["pb"] = held["p"].astype(BF)

    def mix(head, held):
        if load_o is None:
            held["o"] = dot(turned(head, "v", load_v), held["pb"], 1, 0)
        else:
            held["o"] = turned(head, "o", load_o, True)

    def grad_score(head, held):
        row_terms = jnp.sum(held["o"] * turned(head, "do", load_do, True), 0, keepdims=True)
        held["ds"] = (held.pop("p") * (held.pop("dp") - row_terms)).astype(BF)

    def finish(head, held):
        grad = held.pop("ds")
        held["dv"] = dot(held.pop("pb"), held.pop("do"), 1, 0)
        held["dk"] = dot(grad, held.pop("q"), 1, 0)
        held["dq"] = dot(turned(head, "k", load_k), grad, 1, 0) * HEAD**-0.5
        if head % 2 == 0:
            cache["half"] = held
            return
        first = cache.pop("half")
        mixed = None
        if load_o is None:
            mixed = jnp.concatenate([first["o"], held["o"]], 0).astype(BF).T
        query = jnp.concatenate([first["dq"], held["dq"]], 0).astype(BF).T
        store(
            head,
            query,
            (first["dk"] + held["dk"]).astype(BF),
            (first["dv"] + held["dv"]).astype(BF),
            mixed,
        )

    interleave([score, soften, mix, grad_score, finish], HEADS)


def in_hbm(shape, kind):
    return pltpu.HBM(shape, kind)


def bits_of(count):
    return count.bit_length() - 1


def place_to_part(place, order):
    part = 0
    for index, bit in enumerate(order):
        if place >> (len(order) - 1 - index) & 1:
            part |= 1 << bit
    return part


def part_to_place(distance, order):
    place = jnp.int32(0)
    for position, bit in enumerate(order):
        place = place | (((distance >> bit) & 1) << (len(order) - 1 - position))
    return place


def product_block(acc, left, right):
    acc[...] = dot(left[...], right[...], 0, 0).astype(BF)


def put_part(part, distance, order, kept, sent):
    half = kept.shape[0]
    place = part_to_place(distance, order)

    @pl.when(place < half)
    def _():
        kept[jnp.minimum(place, half - 1)] = part

    @pl.when(place >= half)
    def _():
        sent[jnp.maximum(place - half, 0)] = part


def put_parts(acc, own, shards, order, kept, sent):
    part_rows = acc.shape[0] // shards
    half = shards // 2
    for place in range(shards):
        if part_rows % 16:
            part = acc[place * part_rows : (place + 1) * part_rows, :]
            put_part(part, own ^ place, order, kept, sent)
            continue
        owner = own ^ place_to_part(place, order)
        at = pl.ds(pl.multiple_of(owner * part_rows, 16), part_rows)
        if place < half:
            kept[place] = acc[at, :]
        else:
            sent[place - half] = acc[at, :]


def put_parts_tall(acc, own, orders, bounds, outs, block):
    part_rows = outs[0].shape[1]
    per_block = acc.shape[0] // part_rows
    for sub in range(per_block):
        distance = own ^ (block * per_block + sub)
        for kind, order in enumerate(orders):
            kept, sent = outs[2 * kind : 2 * kind + 2]
            part = acc[sub * part_rows : (sub + 1) * part_rows, bounds[kind] : bounds[kind + 1]]
            put_part(part, distance, order, kept, sent)


def part_outs(shards, part_rows, width, bounds, lead):
    half = shards // 2
    specs, shapes = [], []
    for low, high in zip(bounds, bounds[1:]):
        for _ in range(2):

            def index(j, *_, low=low, high=high):
                return (0, 0, jnp.clip(j - lead, low, high - 1) - low)

            specs.append(pl.BlockSpec((half, part_rows, width), index))
            shapes.append(in_hbm((half, part_rows, width * (high - low)), BF))
    return specs, shapes


def pack_clip(cls_ref, clip, source, target, masked):
    start = start_of(cls_ref, clip)

    def copy(rows, live):
        held = min(rows, SLOT)
        value = source[clip * SLOT : clip * SLOT + held, :]
        if masked:
            row = lax.broadcasted_iota(jnp.int32, value.shape, 0)
            value = jnp.where(row < live, value, jnp.zeros_like(value))
        if rows > held:
            pad = jnp.zeros((rows - held, value.shape[1]), value.dtype)
            value = jnp.concatenate([value, pad], 0)
        target[pl.ds(start, rows), :] = value

    by_class(cls_ref[clip], copy)


def call(kernel, scalars, grid, in_specs, operands, after=(), scratch=(), limit=20, **options):
    scalars, operands, after = list(scalars), list(operands), jax.tree.leaves(after)
    known = len(scalars) + len(operands)

    def body(*refs):
        kernel(*refs[:known], *refs[known + len(after) :])

    return pl.pallas_call(
        body,
        grid_spec=pltpu.PrefetchScalarGridSpec(
            num_scalar_prefetch=len(scalars),
            grid=grid,
            in_specs=list(in_specs) + [pl.BlockSpec(memory_space=pl.ANY)] * len(after),
            out_specs=options.pop("out_specs"),
            scratch_shapes=list(scratch),
        ),
        compiler_params=params(limit),
        **options,
    )(*scalars, *operands, *after)


def whole(shape):
    del shape
    return pl.BlockSpec(memory_space=pltpu.VMEM)


def whole_out(shape):
    del shape
    return pl.BlockSpec(memory_space=pltpu.VMEM)


def tile(rows, columns):
    return pl.BlockSpec((rows, columns), lambda i, *_: (i, 0))


def in_main(value):
    return pltpu.with_memory_space_constraint(value, pltpu.HBM)


def pack_grad(cotangent, classes, rows, w_out, after=()):
    clips = classes.shape[0]
    width = cotangent.shape[1]

    def kernel(cls_ref, source, out_w, target, do_ref):
        for clip in range(clips):
            pack_clip(cls_ref, clip, source, target, True)
        clear_tail(cls_ref, clips, [target, do_ref])
        for clip in range(clips):
            start = start_of(cls_ref, clip)

            def body(count, live):
                at = pl.ds(start, count)
                do_ref[at, :] = dot(target[at, :], out_w[...], 1, 1).astype(BF)

            by_class(cls_ref[clip], body)

    return call(
        kernel,
        [classes],
        (1,),
        [whole(cotangent.shape), whole(w_out.shape)],
        [cotangent, w_out],
        after,
        limit=20,
        out_specs=[whole_out((rows, width))] * 2,
        out_shape=[jax.ShapeDtypeStruct((rows, width), BF)] * 2,
        cost_estimate=cost(2 * rows * width * width, 6 * rows * width),
    )


def norm_project(tokens, classes, rows, gain, bias, weight, step, after=()):
    clips = classes.shape[0]
    width, wide = weight.shape

    def kernel(cls_ref, tok_ref, gain_ref, bias_ref, w_ref, x_ref, h_ref, qkv_ref):
        index = pl.program_id(0)

        @pl.when(index == 0)
        def _():
            for clip in range(clips):
                pack_clip(cls_ref, clip, tok_ref, x_ref, False)
            clear_tail(cls_ref, clips, [x_ref])

        live = index * step < total_of(cls_ref, clips)

        @pl.when(live)
        def _():
            at = pl.ds(pl.multiple_of(index * step, 16), step)
            unit, _ = norm_stats(x_ref[at, :].astype(F32))
            low = (unit * gain_ref[:, :width] + bias_ref[:, :width]).astype(BF)
            h_ref[...] = low
            qkv_ref[...] = dot(low, w_ref[...], 1, 0).astype(BF)

        @pl.when(jnp.logical_not(live))
        def _():
            h_ref[...] = jnp.zeros_like(h_ref)
            qkv_ref[...] = jnp.zeros_like(qkv_ref)

    return call(
        kernel,
        [classes],
        (rows // step,),
        [whole(tokens.shape), whole(gain.shape), whole(bias.shape), whole(weight.shape)],
        [tokens, gain, bias, weight],
        after,
        limit=20,
        out_specs=[whole_out((rows, width)), tile(step, width), tile(step, wide)],
        out_shape=[
            jax.ShapeDtypeStruct((rows, width), BF),
            in_hbm((rows, width), BF),
            jax.ShapeDtypeStruct((rows, wide), BF),
        ],
        cost_estimate=cost(2 * rows * width * wide, 2 * rows * (3 * width + wide) + 2 * weight.size),
    )


def self_attend(qkv, classes, after=()):
    clips = classes.shape[0]
    rows, wide = qkv.shape
    width = wide // 3

    def kernel(cls_ref, qkv_ref, o_ref):
        clip = pl.program_id(0)
        start = start_dyn(cls_ref, clip, clips)

        def body(count, live):
            at = pl.ds(start, count)

            def load(part):
                def get(head):
                    pair = pair_of(head)
                    return qkv_ref[at, part * width + pair.start : part * width + pair.stop]

                return get

            def store(head, mixed):
                o_ref[at, pair_of(head)] = mixed

            attend(load(0), load(1), load(2), store, live)

        by_class(cls_ref[clip], body)

        @pl.when(clip == clips - 1)
        def _():
            clear_tail(cls_ref, clips, [o_ref])

    return call(
        kernel,
        [classes],
        (clips,),
        [whole(qkv.shape)],
        [qkv],
        after,
        limit=20,
        out_specs=whole_out((rows, width)),
        out_shape=jax.ShapeDtypeStruct((rows, width), BF),
        cost_estimate=cost(16 * rows * MOST * width, 2 * rows * (wide + width)),
    )


def feed_forward(x, mixed, classes, gains, biases, w_out, w_up, w_down, w_fq, step, tiles, done=None, after=()):
    clips = classes.shape[0]
    rows, width = x.shape
    hidden = w_up.shape[1]
    chunk = width
    first, last = tiles
    shapes = [(width, F32), (width, BF), (hidden, BF), (hidden, BF), (width, F32), (width, BF), (width, BF)]
    count = 0 if done is None else len(shapes)

    def kernel(cls_ref, x_ref, o_ref, gain_ref, bias_ref, out_w, up_w, down_w, fq_w, *refs):
        mid_ref, h_ref, u_ref, act_ref, layer_ref, n_ref, fq_ref, part_ref = refs[count:]
        live = (first + pl.program_id(0)) * step < total_of(cls_ref, clips)

        @pl.when(live)
        def _():
            middle = x_ref[...].astype(F32) + dot(o_ref[...], out_w[...], 1, 0)
            mid_ref[...] = middle
            unit, _ = norm_stats(middle)
            low = (unit * gain_ref[:, width : 2 * width] + bias_ref[:, width : 2 * width]).astype(BF)
            h_ref[...] = low
            layer = middle
            for at in range(0, hidden, chunk):
                part = slice(at, at + chunk)
                up = dot(low, up_w[:, part], 1, 0)
                inner = jnp.tanh(GELU_A * (up + GELU_B * (up * up * up)))
                act = (0.5 * up * (1.0 + inner)).astype(BF)
                u_ref[:, part] = up.astype(BF)
                act_ref[:, part] = act
                layer = layer + dot(act, down_w[part, :], 1, 0)
            layer_ref[...] = layer
            unit, _ = norm_stats(layer)
            low = (unit * gain_ref[:, 2 * width :] + bias_ref[:, 2 * width :]).astype(BF)
            n_ref[...] = low
            part_ref[...] = low
            fq_ref[...] = dot(low, fq_w[...], 1, 0).astype(BF)

        @pl.when(jnp.logical_not(live))
        def _():
            for ref in (mid_ref, h_ref, u_ref, act_ref, layer_ref, n_ref, fq_ref, part_ref):
                ref[...] = jnp.zeros_like(ref)

    weights = [w_out, w_up, w_down, w_fq]
    operands = [classes, x, mixed, gains, biases, *weights] + list(done or [])
    share = (last - first) * step

    def part_tile(columns):
        return pl.BlockSpec((step, columns), lambda i, *_: (first + i, 0))

    return call(
        kernel,
        operands[:1],
        (last - first,),
        [part_tile(width), part_tile(width), whole(gains.shape), whole(biases.shape)]
            + [whole(w.shape) for w in weights]
            + [pl.BlockSpec(memory_space=pl.ANY)] * count,
        operands[1:],
        after,
        limit=20,
        out_specs=[part_tile(columns) for columns, _ in shapes] + [tile(step, width)],
        out_shape=[in_hbm((rows, columns), kind) for columns, kind in shapes] + [in_hbm((share, width), BF)],
        input_output_aliases={len(operands) - count + i: i for i in range(count)},
        cost_estimate=cost(
            2 * share * sum(w.size for w in weights),
            2 * sum(w.size for w in weights) + share * (4 * 5 * width + 4 * hidden),
        ),
    )


def join_attend(arrived, fq, grad_mixed, w_kv, classes, first, last, after=()):
    clips = classes.shape[0]
    rows, width = fq.shape
    wide = w_kv.shape[1]
    parts = len(arrived)
    share = (last - first) * MOST

    def kernel(cls_ref, *refs):
        pieces = refs[:parts]
        q_ref, do_ref, kv_w, o_ref, dq_ref, dn_ref, dkv_ref = refs[parts : parts + 7]
        kv = refs[-1]
        n_ref = refs[parts + 7] if parts > 1 else pieces[0]
        clip = first + pl.program_id(0)
        start = start_dyn(cls_ref, clip, clips)
        base = start_of(cls_ref, first)

        if parts > 1:

            @pl.when(clip == first)
            def _():
                at = 0
                for piece in pieces:
                    n_ref[at : at + piece.shape[0], :] = piece[...]
                    at += piece.shape[0]

        def body(count, live):
            at = pl.ds(start, count)
            to = pl.ds(pl.multiple_of(start - base, 16), count)
            kv[:count, :] = dot(n_ref[at, :], kv_w[...], 1, 0).astype(BF)

            def load_k(head):
                return kv[:count, pair_of(head)]

            def load_v(head):
                pair = pair_of(head)
                return kv[:count, width + pair.start : width + pair.stop]

            def store(head, query, key, value, mixed):
                pair = pair_of(head)
                o_ref[to, pair] = mixed
                dq_ref[to, pair] = query
                dkv_ref[to, pair] = key
                dkv_ref[to, width + pair.start : width + pair.stop] = value

            attend_back(
                lambda head: q_ref[at, pair_of(head)],
                load_k,
                load_v,
                lambda head: do_ref[at, pair_of(head)],
                None,
                store,
                live,
            )
            dn_ref[to, :] = dot(dkv_ref[to, :], kv_w[...], 1, 1).astype(BF)

        by_class(cls_ref[clip], body)

        @pl.when(clip == last - 1)
        def _():
            clear_from(start_of(cls_ref, last) - base, [o_ref, dq_ref, dkv_ref, dn_ref])

    operands = [*arrived, fq, grad_mixed, w_kv]
    return call(
        kernel,
        [classes],
        (last - first,),
        [whole(v.shape) for v in operands],
        [*operands],
        after,
        limit=24,
        out_specs=[whole_out((share, width))] * (4 if parts == 1 else 5),
        scratch=[pltpu.VMEM((MOST, wide), BF)],
        out_shape=[
            in_hbm((share, width), BF), in_hbm((share, width), BF), jax.ShapeDtypeStruct((share, width), BF),
            in_hbm((share, wide), BF),
        ]
        + ([jax.ShapeDtypeStruct((rows, width), BF)] if parts > 1 else []),
        cost_estimate=cost(32 * rows * MOST * width, 10 * rows * width),
    )


def join_weights(own, products, classes, shards, order, after=()):
    clips = classes.shape[0]
    flat, places = [], []

    def place(value):
        for at, held in enumerate(flat):
            if held is value:
                return at
        flat.append(value)
        return len(flat) - 1

    for left, right, column in products:
        places.append(([place(v) for v in left], [place(v) for v in right], column))
    width = products[0][0][0].shape[1]
    share = min(v.shape[0] for v in flat)
    specs, shapes = part_outs(shards, width // shards, width, [0, len(products)], 0)

    def kernel(cls_ref, own_ref, *refs):
        kept, sent, acc = refs[-3:]
        index = pl.program_id(0)
        tail = pl.ds(start_of(cls_ref, clips // 2), share)

        def pieces(at, column):
            part = slice(column * width, (column + 1) * width)
            if len(at) == 2:
                return refs[at[0]][:, part], refs[at[1]][:, part]
            return refs[at[0]][:share, part], refs[at[0]][tail, part]

        for block, (left, right, column) in enumerate(places):

            @pl.when(index == block)
            def _():
                left_head, left_tail = pieces(left, 0)
                right_head, right_tail = pieces(right, column)
                acc[...] = (dot(left_head, right_head, 0, 0) + dot(left_tail, right_tail, 0, 0)).astype(BF)

        put_parts(acc, own_ref[0], shards, order, kept, sent)

    out = call(
        kernel,
        [classes, own],
        (len(products),),
        [whole(v.shape) for v in flat],
        flat,
        after,
        limit=24,
        out_specs=specs,
        scratch=[pltpu.VMEM((width, width), BF)],
        out_shape=shapes,
        cost_estimate=cost(2 * share * width * width, 4 * share * width),
    )
    return Sum(*out, order)


def join_result(layer, mixed, w_out, classes, slots, after=()):
    clips = classes.shape[0]
    rows, width = layer.shape

    def kernel(cls_ref, layer_ref, oa, ob, w_ref, out_ref):
        for clip in range(clips):
            start = start_of(cls_ref, clip)
            o_ref = oa if clip < clips // 2 else ob
            base = 0 if clip < clips // 2 else start_of(cls_ref, clips // 2)

            def body(count, live, start=start, base=base, o_ref=o_ref, clip=clip):
                at = pl.ds(start, count)
                from_at = pl.ds(pl.multiple_of(start - base, 16), count)
                value = layer_ref[at, :] + dot(o_ref[from_at, :], w_ref[...], 1, 0)
                held = min(count, SLOT)
                row = lax.broadcasted_iota(jnp.int32, value.shape, 0)
                value = jnp.where(row < live, value, 0.0).astype(BF)
                first = clip * SLOT
                out_ref[first : first + held, :] = value[:held]
                if held < SLOT:
                    out_ref[first + held : first + SLOT, :] = jnp.zeros((SLOT - held, width), BF)

            by_class(cls_ref[clip], body)

    return call(
        kernel,
        [classes],
        (1,),
        [whole(v.shape) for v in (layer, *mixed, w_out)],
        [layer, *mixed, w_out],
        after,
        limit=20,
        out_specs=whole_out((slots, width)),
        out_shape=jax.ShapeDtypeStruct((slots, width), BF),
        cost_estimate=cost(2 * rows * width * width, 8 * rows * width + 2 * w_out.size),
    )


def join_back(own, dfq, back, layer, grad, act, classes, gains, w_fq, step, shards, orders, cuts, after=()):
    clips = classes.shape[0]
    rows, width = layer.shape
    tall = act.shape[1]
    blocks = tall // width
    tiles = rows // step
    bounds = [*cuts, width]
    half = shards // 2
    outs_shapes = [
        jax.ShapeDtypeStruct((half, tall // shards, bounds[k + 1] - bounds[k]), BF) for k in range(len(orders)) for _ in range(2)
    ]

    def kernel(
        cls_ref, own_ref, dfqa, dfqb, backa, backb, layer_ref, g_ref, act_ref, gain_ref, fq_w,
        out_ref, gain_acc, bias_acc, *refs,
    ):
        outs = refs[:-4]
        dfq_ref, back_ref, low_ref, acc = refs[-4:]
        index = pl.program_id(0)

        @pl.when(index == 0)
        def _():
            gain_acc[...] = jnp.zeros_like(gain_acc)
            bias_acc[...] = jnp.zeros_like(bias_acc)
            base = start_of(cls_ref, clips // 2)
            merge(dfqa, dfqb, base, dfq_ref)
            merge(backa, backb, base, back_ref)

        total = total_of(cls_ref, clips)
        live = index * step < total
        at = pl.ds(pl.multiple_of(jnp.minimum(index, tiles - 1) * step, 16), step)

        @pl.when((index < tiles) & live)
        def _():
            grad_norm = dot(dfq_ref[at, :], fq_w[...], 1, 1) + back_ref[at, :].astype(F32)
            grad_layer = g_ref[...].astype(F32) + norm_back(
                layer_ref[...], gain_ref[:, 2 * width :], grad_norm, gain_acc, bias_acc
            )
            out_ref[...] = grad_layer
            low_ref[at, :] = grad_layer.astype(BF)

        @pl.when((index < tiles) & jnp.logical_not(live))
        def _():
            out_ref[...] = jnp.zeros_like(out_ref)
            low_ref[at, :] = jnp.zeros((step, width), BF)

        @pl.when(index >= tiles)
        def _():
            product_block(acc, act_ref, low_ref)
            put_parts_tall(acc, own_ref[0], orders, bounds, outs, index - tiles)

    def row_tile(columns):
        return pl.BlockSpec((step, columns), lambda i, *_: (jnp.minimum(i, tiles - 1), 0))

    out = call(
        kernel,
        [classes, own],
        (tiles + blocks,),
        [whole(v.shape) for v in (*dfq, *back)]
            + [row_tile(width)] * 2
            + [pl.BlockSpec((rows, width), lambda i, *_: (0, jnp.maximum(i - tiles, 0)))]
            + [whole(gains.shape), whole(w_fq.shape)],
        [*dfq, *back, layer, grad, act, gains, w_fq],
        after,
        limit=20,
        out_specs=[row_tile(width)] + [whole_out((1, width))] * 2 + [whole_out(v.shape) for v in outs_shapes],
            scratch=[pltpu.VMEM((rows, width), BF)] * 3 + [pltpu.VMEM((width, width), BF)],
        out_shape=[jax.ShapeDtypeStruct((rows, width), F32)]
        + [jax.ShapeDtypeStruct((1, width), F32)] * 2
        + outs_shapes,
        cost_estimate=cost(2 * rows * width * (width + tall), 16 * rows * width + 2 * act.size + 2 * tall * width),
    )
    return *out[:3], *(Sum(*out[3 + 2 * k : 5 + 2 * k], order) for k, order in enumerate(orders))


def feed_forward_back(grad_layer, up, middle, classes, gains, w_down, w_up, w_out, step, after=()):
    clips = classes.shape[0]
    rows, width = middle.shape
    hidden = w_up.shape[1]
    chunk = width
    blocks = hidden // width

    def kernel(
        cls_ref, g_ref, u_ref, mid_ref, gain_ref, down_w, up_w, out_w,
        gmid_ref, low_ref, do_ref, hid_ref, gain_acc, bias_acc,
    ):
        index = pl.program_id(0)

        @pl.when(index == 0)
        def _():
            gain_acc[...] = jnp.zeros_like(gain_acc)
            bias_acc[...] = jnp.zeros_like(bias_acc)

        live = index * step < total_of(cls_ref, clips)

        @pl.when(live)
        def _():
            grad_layer = g_ref[...]
            down_low = grad_layer.astype(BF)
            total_norm = [jnp.zeros((step, width), F32)]

            def act_stage(k, held):
                held["g"] = dot(down_low, down_w[k * chunk : (k + 1) * chunk, :], 1, 1)

            def slope_stage(k, held):
                part = slice(k * chunk, (k + 1) * chunk)
                value = u_ref[:, part].astype(F32)
                square = value * value
                inner = jnp.tanh(value * (GELU_A + (GELU_A * GELU_B) * square))
                slope = (0.5 + 0.5 * inner) + value * (1.0 - inner * inner) * (
                    0.5 * GELU_A + (1.5 * GELU_A * GELU_B) * square
                )
                held["l"] = (held.pop("g") * slope).astype(BF)
                hid_ref[:, part] = held["l"]

            def norm_stage(k, held):
                total_norm[0] += dot(held.pop("l"), up_w[:, k * chunk : (k + 1) * chunk], 1, 1)

            interleave([act_stage, slope_stage, norm_stage], blocks)
            grad_middle = grad_layer + norm_back(
                mid_ref[...], gain_ref[:, width : 2 * width], total_norm[0], gain_acc, bias_acc
            )
            gmid_ref[...] = grad_middle
            low = grad_middle.astype(BF)
            low_ref[...] = low
            do_ref[...] = dot(low, out_w[...], 1, 1).astype(BF)

        @pl.when(jnp.logical_not(live))
        def _():
            for ref in (gmid_ref, low_ref, do_ref, hid_ref):
                ref[...] = jnp.zeros_like(ref)

    weights = [w_down, w_up, w_out]
    return call(
        kernel,
        [classes],
        (rows // step,),
        [tile(step, width), tile(step, hidden), tile(step, width), whole(gains.shape)]
            + [whole(w.shape) for w in weights],
        [grad_layer, up, middle, gains, *weights],
        after,
        limit=22,
        out_specs=[tile(step, width)] * 3 + [tile(step, hidden)] + [whole_out((1, width))] * 2,
        out_shape=[
            in_hbm((rows, width), F32),
            in_hbm((rows, width), BF),
            jax.ShapeDtypeStruct((rows, width), BF),
            in_hbm((rows, hidden), BF),
        ]
        + [jax.ShapeDtypeStruct((1, width), F32)] * 2,
        cost_estimate=cost(2 * rows * sum(w.size for w in weights), 2 * sum(w.size for w in weights)),
    )


def feed_forward_weights(own, normed, hidden_low, mixed, out_low, shards, orders, cut, after=()):
    rows, width = normed.shape
    blocks = hidden_low.shape[1] // width
    bounds = [0, cut, blocks + 1][: len(orders)] + [blocks + 1]
    specs, shapes = part_outs(shards, width // shards, width, bounds, 0)

    def kernel(own_ref, n_ref, hid_ref, o_ref, low_ref, *refs):
        outs, acc = refs[:-1], refs[-1]
        block = pl.program_id(0)

        @pl.when(block < blocks)
        def _():
            product_block(acc, n_ref, hid_ref)

        @pl.when(block == blocks)
        def _():
            product_block(acc, o_ref, low_ref)

        for kind, order in enumerate(orders):

            @pl.when((block >= bounds[kind]) & (block < bounds[kind + 1]))
            def _():
                put_parts(acc, own_ref[0], shards, order, *outs[2 * kind : 2 * kind + 2])

    out = call(
        kernel,
        [own],
        (blocks + 1,),
        [
                whole(normed.shape),
                pl.BlockSpec((rows, width), lambda j, *_: (0, jnp.minimum(j, blocks - 1))),
                whole(mixed.shape),
                whole(out_low.shape),
            ],
        [normed, hidden_low, mixed, out_low],
        after,
        limit=20,
        out_specs=specs,
            scratch=[pltpu.VMEM((width, width), BF)],
        out_shape=shapes,
        cost_estimate=cost(2 * rows * width * width * (blocks + 1), 2 * rows * width * 8),
    )
    return [Sum(*out[2 * k : 2 * k + 2], order) for k, order in enumerate(orders)]


def self_attend_back(own, qkv, mixed, grad, normed, classes, shards, orders, cut, after=()):
    clips = classes.shape[0]
    rows, wide = qkv.shape
    width = wide // 3
    bounds = [0, cut, 3]
    specs, shapes = part_outs(shards, width // shards, width, bounds, clips)

    def kernel(cls_ref, own_ref, qkv_ref, o_ref, do_ref, n_ref, d_ref, *refs):
        outs = refs[:4]
        acc = refs[4]
        index = pl.program_id(0)

        @pl.when(index < clips)
        def _():
            clip = jnp.minimum(index, clips - 1)
            start = start_dyn(cls_ref, clip, clips)

            def body(count, live):
                at = pl.ds(start, count)

                def columns(part, head):
                    pair = pair_of(head)
                    return slice(part * width + pair.start, part * width + pair.stop)

                def load(part):
                    return lambda head: qkv_ref[at, columns(part, head)]

                def store(head, query, key, value, _):
                    for part, result in enumerate((query, key, value)):
                        d_ref[at, columns(part, head)] = result

                attend_back(
                    load(0),
                    load(1),
                    load(2),
                    lambda head: do_ref[at, pair_of(head)],
                    lambda head: o_ref[at, pair_of(head)],
                    store,
                    live,
                )

            by_class(cls_ref[clip], body)

        @pl.when(index == clips - 1)
        def _():
            clear_tail(cls_ref, clips, [d_ref])

        products = [(n_ref, d_ref.at[:, p * width : (p + 1) * width]) for p in range(3)]
        for block, (left, right) in enumerate(products):

            @pl.when(index == clips + block)
            def _():
                product_block(acc, left, right)
                kind = 0 if block < cut else 1
                put_parts(acc, own_ref[0], shards, orders[kind], *outs[2 * kind : 2 * kind + 2])

    operands = [qkv, mixed, grad, normed]
    out = call(
        kernel,
        [classes, own],
        (clips + 3,),
        [whole(v.shape) for v in operands],
        [*operands],
        after,
        limit=20,
        out_specs=[whole_out((rows, wide))] + specs,
            scratch=[pltpu.VMEM((width, width), BF)],
        out_shape=[jax.ShapeDtypeStruct((rows, wide), BF)] + shapes,
        cost_estimate=cost(48 * rows * MOST * width, 16 * rows * width),
    )
    return out[0], Sum(*out[1:3], orders[0]), Sum(*out[3:5], orders[1])


def norm_project_back(dqkv, x, gmid, classes, gain, weight, step, slots, after=()):
    clips = classes.shape[0]
    rows, width = x.shape
    wide = weight.shape[1]

    def kernel(cls_ref, d_ref, x_ref, gmid_ref, gain_ref, w_ref, out_ref, gain_one, bias_one, packed):
        index = pl.program_id(0)

        @pl.when(index == 0)
        def _():
            gain_one[...] = jnp.zeros_like(gain_one)
            bias_one[...] = jnp.zeros_like(bias_one)

        @pl.when(index * step < total_of(cls_ref, clips))
        def _():
            grad_norm = dot(d_ref[...], w_ref[...], 1, 1)
            at = pl.ds(pl.multiple_of(index * step, 16), step)
            packed[at, :] = gmid_ref[...] + norm_back(
                x_ref[...].astype(F32), gain_ref[:, :width], grad_norm, gain_one, bias_one
            )

        @pl.when(index == rows // step - 1)
        def _():
            for clip in range(clips):
                start = start_of(cls_ref, clip)

                def body(count, live):
                    value = packed[pl.ds(start, count), :]
                    held = min(count, SLOT)
                    first = clip * SLOT
                    out_ref[first : first + held, :] = value[:held]
                    if held < SLOT:
                        out_ref[first + held : first + SLOT, :] = jnp.zeros((SLOT - held, width), F32)

                by_class(cls_ref[clip], body)

    return call(
        kernel,
        [classes],
        (rows // step,),
        [
                tile(step, wide), tile(step, width), tile(step, width), whole(gain.shape), whole(weight.shape),
            ],
        [dqkv, x, gmid, gain, weight],
        after,
        limit=20,
        out_specs=[whole_out((slots, width))] + [whole_out((1, width))] * 2,
            scratch=[pltpu.VMEM((rows, width), F32)],
        out_shape=[jax.ShapeDtypeStruct((slots, width), F32)] + [jax.ShapeDtypeStruct((1, width), F32)] * 2,
        cost_estimate=cost(2 * rows * width * wide, rows * (10 * width + 2 * wide) + 2 * weight.size),
    )


def exchange(value, bit):
    count = lax.axis_size("dp")
    return lax.ppermute(value, "dp", [(i, i ^ (1 << bit)) for i in range(count)])


def tie(values, *before):
    return lax.optimization_barrier((values, before))[0]


class Sum:
    def __init__(self, kept, sent, order):
        self.kept, self.sent, self.order, self.step = kept, sent, order, 0
        self.got = None

    def start(self):
        self.got = exchange(self.sent, self.order[self.step])

    def add(self, *before, go=True):
        if self.step == len(self.order):
            return self.result
        kept, got, self.got = self.kept, self.got, None
        if before:
            kept, got = tie((kept, got), *before)
        self.step += 1
        if self.step == len(self.order):
            self.result = kept[0].astype(F32) + got[0].astype(F32)
            return self.result
        half = kept.shape[0] // 2
        self.sent = (kept[half:].astype(F32) + got[half:].astype(F32)).astype(kept.dtype)
        self.kept = (kept[:half].astype(F32) + got[:half].astype(F32)).astype(kept.dtype)
        if go:
            self.start()
        return self.sent, self.kept


def take_turns(sums, last):
    for one in sums:
        if one.got is None:
            one.start()
        else:
            last = one.add(last)
    return last


def shifted(value, axis, steps):
    count = lax.axis_size(axis)
    return lax.ppermute(value, axis, [(source, (source + steps) % count) for source in range(count)])


def per_device(
    tokens, item_class, norm_gain, norm_bias, attn_qkv, attn_out, mlp_up, mlp_down,
    join_query, join_keyval, join_output, cotangent,
):
    width = tokens.shape[2]
    slots = tokens.shape[1]
    clips = item_class.shape[0]
    rows = clips * MOST
    shards = lax.axis_size("dp")
    step, small_step = MOST, MOST * 2 // 3
    w_qkv, w_out, w_up, w_down = attn_qkv[0], attn_out[0], mlp_up[0], mlp_down[0]
    w_fq, w_fkv, w_fo = join_query[0], join_keyval[0], join_output[0]
    own = lax.axis_index("dp").astype(jnp.int32)[None]

    next_fkv = shifted(w_fkv, "view", -1)
    norm_gain, norm_bias = norm_gain.reshape(1, -1), norm_bias.reshape(1, -1)
    x, low_one, qkv = norm_project(tokens[0], item_class, rows, norm_gain, norm_bias, w_qkv, step)
    mixed = self_attend(qkv, item_class)
    tiles = rows // small_step
    args = (x, mixed, item_class, norm_gain, norm_bias, w_out, w_up, w_down, w_fq, small_step)
    *done, part_a = feed_forward(*args, (0, tiles // 2))
    arrived_a = shifted(part_a, "view", -1)
    *done, part_b = feed_forward(*args, (tiles // 2, tiles), done)
    arrived_b = shifted(part_b, "view", -1)
    middle, low_two, up, act, layer, low_three, fq = done
    grad, grad_mixed = pack_grad(cotangent[0], item_class, rows, w_fo, after=(part_b, arrived_a))

    bits = range(bits_of(shards))
    orders = tuple(bits), (*bits[1::-1], *bits[2:])
    half = clips // 2
    join_args = (fq, grad_mixed, next_fkv, item_class)
    mixed_a, dfq_a, back_a, dkv_a = join_attend((arrived_a,), *join_args, 0, half)
    returned_a = shifted(back_a, "view", 1)
    mixed_b, dfq_b, back_b, dkv_b, arrived = join_attend((arrived_a, arrived_b), *join_args, half, clips, after=back_a)
    returned_b = shifted(back_b, "view", 1)
    join_mixed, dfq = (mixed_a, mixed_b), (dfq_a, dfq_b)
    by_y, by_z = orders
    dkv = (dkv_a, dkv_b)
    join_y = join_weights(
        own, [((arrived,), dkv, 0), ((arrived,), dkv, 1)], item_class, shards, by_y, after=returned_a
    )
    join_y.start()
    join_z = join_weights(
        own, [((low_three,), dfq, 0), (join_mixed, (grad,), 0)], item_class, shards, by_z,
        after=(join_y.kept, returned_b),
    )
    join_z.start()
    joined = join_result(layer, join_mixed, w_fo, item_class, slots, after=join_z.kept)
    grad_layer, gain_three, bias_three, down_y, down_z = join_back(
        own, dfq, (returned_a, returned_b), layer, grad, in_main(act), item_class, norm_gain, w_fq,
        step, shards, orders, (0, width // 2), after=joined,
    )
    down_y.start()
    down_z.start()
    last = [one.add(gain_three) for one in (join_y, join_z)]
    gmid, out_low, do_self, hidden_low, gain_two, bias_two = feed_forward_back(
        grad_layer, in_main(up), middle, item_class, norm_gain, w_down, w_up, w_out, small_step, after=last
    )
    last = [one.add(gain_two, go=False) for one in (join_y, join_z)]
    last += [one.add(gain_two) for one in (down_y, down_z)]
    up_y, up_z = feed_forward_weights(
        own, low_two, in_main(hidden_low), mixed, out_low, shards, orders, 3, after=last
    )
    up_y.start()
    up_z.start()
    join_y.start()
    dqkv, self_y, self_z = self_attend_back(
        own, qkv, mixed, do_self, low_one, item_class, shards, orders, 2, after=up_y.kept
    )
    self_y.start()
    self_z.start()
    last = join_y.add(self_y.kept)
    join_z.start()
    last = [one.add(last, go=False) for one in (down_y, down_z)]
    grad_tokens, gain_one, bias_one = norm_project_back(
        dqkv, x, gmid, item_class, norm_gain, w_qkv, step, slots, after=last
    )
    small = jnp.concatenate([gain_one, gain_two, gain_three, bias_one, bias_two, bias_three], 0)
    small = small.reshape(6, shards, width // shards).transpose(1, 0, 2)
    small = jnp.stack([small[own[0] ^ place_to_part(place, tuple(bits))] for place in range(shards)])
    small = Sum(small[: shards // 2], small[shards // 2 :], tuple(bits))
    last = take_turns(
        (up_z, up_y, join_z, down_y, self_z, self_y, down_y, down_z, up_z, up_y, self_z, self_y, down_z), gain_one
    )
    small.sent = tie(small.sent, last)
    last = take_turns((small, up_z, small, up_y, small, self_z, self_y, small), last)
    for _ in bits[3:]:
        last = [one.add() for one in (join_y, join_z, down_y, down_z, up_y, up_z, self_y, self_z, small)]
    sum_fkv = shifted(tie(join_y.result, gain_one), "view", 1)
    return (
        joined[None],
        grad_tokens[None],
        small.result[None, :3],
        small.result[None, 3:],
        jnp.concatenate([self_y.result, self_z.result], 1)[None],
        up_z.result[None, :, width:],
        jnp.concatenate([up_y.result, up_z.result[:, :width]], 1)[None],
        jnp.concatenate([down_y.result, down_z.result], 1)[None],
        join_z.result[None, :, :width],
        sum_fkv[None],
        join_z.result[None, :, width:],
    )


def solution(mesh):
    weight = P("view", None, None)
    tokens = P("view", "dp", None)
    small = P("view", None, "dp")
    return jax.shard_map(
        per_device,
        mesh=mesh,
        in_specs=(tokens, P("dp")) + (weight,) * 9 + (tokens,),
        out_specs=(tokens, tokens, small, small) + (tokens,) * 7,
        check_vma=False,
    )
```

```python
import functools

import jax
import jax.numpy as jnp
from jax import lax
from jax.experimental import pallas as pl
from jax.experimental.pallas import tpu as pltpu
from jax.sharding import PartitionSpec as P

HEADS = 12
HEAD = 64
SLOT = 324
CLASSES = ((112, 100), (208, 196), (336, 324))
MOST = 336
EPS = 1e-05
GELU_A = 0.7978845608028654
GELU_B = 0.044715
BF = jnp.bfloat16
F32 = jnp.float32


def dot(left, right, left_dim, right_dim):
    return lax.dot_general(
        left, right, (((left_dim,), (right_dim,)), ((), ())), preferred_element_type=F32
    )


def params(limit_mib=20):
    return pltpu.CompilerParams(vmem_limit_bytes=limit_mib * 2**20)


def cost(flops, moved):
    return pl.CostEstimate(flops=int(flops) // 2000, bytes_accessed=int(moved) // 2000, transcendentals=0)


def rows_of(item):
    return 112 + jnp.where(item >= 1, 96, 0) + jnp.where(item >= 2, 128, 0)


def start_of(cls_ref, clip):
    start = jnp.int32(0)
    for before in range(clip):
        start = start + rows_of(cls_ref[before])
    return pl.multiple_of(start, 16)


def start_dyn(cls_ref, clip, clips):
    start = jnp.int32(0)
    for before in range(clips):
        start = start + jnp.where(before < clip, rows_of(cls_ref[before]), 0)
    return pl.multiple_of(start, 16)


def total_of(cls_ref, clips):
    return start_of(cls_ref, clips)


def clear_from(total, refs):
    rows = refs[0].shape[0]

    @pl.loop(0, (rows - total) // 16)
    def _(step):
        at = pl.ds(pl.multiple_of(total + step * 16, 16), 16)
        for ref in refs:
            ref[at, :] = jnp.zeros((16, ref.shape[1]), ref.dtype)


def clear_tail(cls_ref, clips, refs):
    clear_from(total_of(cls_ref, clips), refs)


def merge(first, second, base, target):
    half = first.shape[0]
    target[:half, :] = first[...]
    target[half:, :] = jnp.zeros((target.shape[0] - half, target.shape[1]), target.dtype)
    target[pl.ds(base, half), :] = second[...]


def by_class(item, body):
    for index, (rows, live) in enumerate(CLASSES):
        pl.when(item == index)(functools.partial(body, rows, live))


def norm_stats(values):
    centre = jnp.mean(values, -1, keepdims=True)
    centred = values - centre
    spread = jnp.mean(centred * centred, -1, keepdims=True)
    root = lax.rsqrt(spread + EPS)
    return centred * root, root


def norm_back(values, gain, grad, gain_acc, bias_acc):
    unit, root = norm_stats(values)
    gain_acc[...] += jnp.sum(grad * unit, 0, keepdims=True)
    bias_acc[...] += jnp.sum(grad, 0, keepdims=True)
    scaled = grad * gain
    return root * (
        scaled
        - jnp.mean(scaled, -1, keepdims=True)
        - unit * jnp.mean(scaled * unit, -1, keepdims=True)
    )


def interleave(stages, count):
    held = [dict() for _ in range(count)]
    for step in range(count + len(stages) - 1):
        for index, stage in enumerate(stages):
            if 0 <= step - index < count:
                stage(step - index, held[step - index])


def one_head(pair, head):
    lane = lax.broadcasted_iota(jnp.int32, pair.shape, 1)
    keep = lane < HEAD if head % 2 == 0 else lane >= HEAD
    return jnp.where(keep, pair, jnp.zeros_like(pair))


def pair_of(head):
    return slice(128 * (head // 2), 128 * (head // 2) + 128)


def mask_keys_lane(scores, live):
    lane = lax.broadcasted_iota(jnp.int32, scores.shape, 1)
    return jnp.where(lane < live, scores, -1e30)


def mask_keys_row(scores, live):
    head, tail = scores[:-16], scores[-16:]
    row = lax.broadcasted_iota(jnp.int32, tail.shape, 0)
    tail = jnp.where(row < live - head.shape[0], tail, -1e30)
    return jnp.concatenate([head, tail], axis=0)


def attend(load_q, load_k, load_v, store, live):
    pairs = {}

    def score(head, held):
        query = one_head(load_q(head), head) * jnp.asarray(HEAD**-0.5, BF)
        held["s"] = mask_keys_lane(dot(query, load_k(head), 1, 1), live)

    def soften(head, held):
        scores = held.pop("s")
        exps = jnp.exp(scores - jnp.max(scores, -1, keepdims=True))
        held["l"] = jnp.sum(exps, -1, keepdims=True)
        held["e"] = exps.astype(BF)

    def mix(head, held):
        mixed = dot(held.pop("e"), one_head(load_v(head), head), 1, 0) / held.pop("l")
        if head % 2 == 0:
            pairs[head // 2] = mixed
        else:
            store(head, (pairs.pop(head // 2) + mixed).astype(BF))

    interleave([score, soften, mix], HEADS)


def attend_back(load_q, load_k, load_v, load_do, load_o, store, live):
    cache = {}

    def turned(head, name, load, wide=False):
        key = (name, head // 2)
        if key not in cache:
            value = load(head).T
            cache[key] = value.astype(F32) if wide else value
        at = HEAD * (head % 2)
        return cache[key][at : at + HEAD]

    def score(head, held):
        held["q"] = one_head(load_q(head), head) * jnp.asarray(HEAD**-0.5, BF)
        held["s"] = mask_keys_row(dot(load_k(head), held["q"], 1, 1), live)
        held["do"] = one_head(load_do(head), head)
        held["dp"] = dot(load_v(head), held["do"], 1, 1)

    def soften(head, held):
        scores = held.pop("s")
        exps = jnp.exp(scores - jnp.max(scores, 0, keepdims=True))
        held["p"] = exps * (1.0 / jnp.sum(exps, 0, keepdims=True))
        held["pb"] = held["p"].astype(BF)

    def mix(head, held):
        if load_o is None:
            held["o"] = dot(turned(head, "v", load_v), held["pb"], 1, 0)
        else:
            held["o"] = turned(head, "o", load_o, True)

    def grad_score(head, held):
        row_terms = jnp.sum(held["o"] * turned(head, "do", load_do, True), 0, keepdims=True)
        held["ds"] = (held.pop("p") * (held.pop("dp") - row_terms)).astype(BF)

    def finish(head, held):
        grad = held.pop("ds")
        held["dv"] = dot(held.pop("pb"), held.pop("do"), 1, 0)
        held["dk"] = dot(grad, held.pop("q"), 1, 0)
        held["dq"] = dot(turned(head, "k", load_k), grad, 1, 0) * HEAD**-0.5
        if head % 2 == 0:
            cache["half"] = held
            return
        first = cache.pop("half")
        mixed = None
        if load_o is None:
            mixed = jnp.concatenate([first["o"], held["o"]], 0).astype(BF).T
        query = jnp.concatenate([first["dq"], held["dq"]], 0).astype(BF).T
        store(
            head,
            query,
            (first["dk"] + held["dk"]).astype(BF),
            (first["dv"] + held["dv"]).astype(BF),
            mixed,
        )

    interleave([score, soften, mix, grad_score, finish], HEADS)


def in_hbm(shape, kind):
    return pltpu.HBM(shape, kind)


def bits_of(count):
    return count.bit_length() - 1


def place_to_part(place, order):
    part = 0
    for index, bit in enumerate(order):
        if place >> (len(order) - 1 - index) & 1:
            part |= 1 << bit
    return part


def part_to_place(distance, order):
    place = jnp.int32(0)
    for position, bit in enumerate(order):
        place = place | (((distance >> bit) & 1) << (len(order) - 1 - position))
    return place


def product_block(acc, left, right):
    acc[...] = dot(left[...], right[...], 0, 0).astype(BF)


def put_part(part, distance, order, kept, sent):
    half = kept.shape[0]
    place = part_to_place(distance, order)

    @pl.when(place < half)
    def _():
        kept[jnp.minimum(place, half - 1)] = part

    @pl.when(place >= half)
    def _():
        sent[jnp.maximum(place - half, 0)] = part


def put_parts(acc, own, shards, order, kept, sent):
    part_rows = acc.shape[0] // shards
    half = shards // 2
    for place in range(shards):
        if part_rows % 16:
            part = acc[place * part_rows : (place + 1) * part_rows, :]
            put_part(part, own ^ place, order, kept, sent)
            continue
        owner = own ^ place_to_part(place, order)
        at = pl.ds(pl.multiple_of(owner * part_rows, 16), part_rows)
        if place < half:
            kept[place] = acc[at, :]
        else:
            sent[place - half] = acc[at, :]


def put_parts_tall(acc, own, orders, bounds, outs, block):
    part_rows = outs[0].shape[1]
    per_block = acc.shape[0] // part_rows
    for sub in range(per_block):
        distance = own ^ (block * per_block + sub)
        for kind, order in enumerate(orders):
            kept, sent = outs[2 * kind : 2 * kind + 2]
            part = acc[sub * part_rows : (sub + 1) * part_rows, bounds[kind] : bounds[kind + 1]]
            put_part(part, distance, order, kept, sent)


def part_outs(shards, part_rows, width, bounds, lead):
    half = shards // 2
    specs, shapes = [], []
    for low, high in zip(bounds, bounds[1:]):
        for _ in range(2):

            def index(j, *_, low=low, high=high):
                return (0, 0, jnp.clip(j - lead, low, high - 1) - low)

            specs.append(pl.BlockSpec((half, part_rows, width), index))
            shapes.append(in_hbm((half, part_rows, width * (high - low)), BF))
    return specs, shapes


def pack_clip(cls_ref, clip, source, target, masked):
    start = start_of(cls_ref, clip)

    def copy(rows, live):
        held = min(rows, SLOT)
        value = source[clip * SLOT : clip * SLOT + held, :]
        if masked:
            row = lax.broadcasted_iota(jnp.int32, value.shape, 0)
            value = jnp.where(row < live, value, jnp.zeros_like(value))
        if rows > held:
            pad = jnp.zeros((rows - held, value.shape[1]), value.dtype)
            value = jnp.concatenate([value, pad], 0)
        target[pl.ds(start, rows), :] = value

    by_class(cls_ref[clip], copy)


def call(kernel, scalars, grid, in_specs, operands, after=(), scratch=(), limit=20, **options):
    scalars, operands, after = list(scalars), list(operands), jax.tree.leaves(after)
    known = len(scalars) + len(operands)

    def body(*refs):
        kernel(*refs[:known], *refs[known + len(after) :])

    return pl.pallas_call(
        body,
        grid_spec=pltpu.PrefetchScalarGridSpec(
            num_scalar_prefetch=len(scalars),
            grid=grid,
            in_specs=list(in_specs) + [pl.BlockSpec(memory_space=pl.ANY)] * len(after),
            out_specs=options.pop("out_specs"),
            scratch_shapes=list(scratch),
        ),
        compiler_params=params(limit),
        **options,
    )(*scalars, *operands, *after)


def whole(shape):
    del shape
    return pl.BlockSpec(memory_space=pltpu.VMEM)


def whole_out(shape):
    del shape
    return pl.BlockSpec(memory_space=pltpu.VMEM)


def tile(rows, columns):
    return pl.BlockSpec((rows, columns), lambda i, *_: (i, 0))


def in_main(value):
    return pltpu.with_memory_space_constraint(value, pltpu.HBM)


def pack_grad(cotangent, classes, rows, w_out, after=()):
    clips = classes.shape[0]
    width = cotangent.shape[1]

    def kernel(cls_ref, source, out_w, target, do_ref):
        for clip in range(clips):
            pack_clip(cls_ref, clip, source, target, True)
        clear_tail(cls_ref, clips, [target, do_ref])
        for clip in range(clips):
            start = start_of(cls_ref, clip)

            def body(count, live):
                at = pl.ds(start, count)
                do_ref[at, :] = dot(target[at, :], out_w[...], 1, 1).astype(BF)

            by_class(cls_ref[clip], body)

    return call(
        kernel,
        [classes],
        (1,),
        [whole(cotangent.shape), whole(w_out.shape)],
        [cotangent, w_out],
        after,
        limit=20,
        out_specs=[whole_out((rows, width))] * 2,
        out_shape=[jax.ShapeDtypeStruct((rows, width), BF)] * 2,
        cost_estimate=cost(2 * rows * width * width, 6 * rows * width),
    )


def norm_project(tokens, classes, rows, gain, bias, weight, step, after=()):
    clips = classes.shape[0]
    width, wide = weight.shape

    def kernel(cls_ref, tok_ref, gain_ref, bias_ref, w_ref, x_ref, h_ref, qkv_ref):
        index = pl.program_id(0)

        @pl.when(index == 0)
        def _():
            for clip in range(clips):
                pack_clip(cls_ref, clip, tok_ref, x_ref, False)
            clear_tail(cls_ref, clips, [x_ref])

        live = index * step < total_of(cls_ref, clips)

        @pl.when(live)
        def _():
            at = pl.ds(pl.multiple_of(index * step, 16), step)
            unit, _ = norm_stats(x_ref[at, :].astype(F32))
            low = (unit * gain_ref[:, :width] + bias_ref[:, :width]).astype(BF)
            h_ref[...] = low
            qkv_ref[...] = dot(low, w_ref[...], 1, 0).astype(BF)

        @pl.when(jnp.logical_not(live))
        def _():
            h_ref[...] = jnp.zeros_like(h_ref)
            qkv_ref[...] = jnp.zeros_like(qkv_ref)

    return call(
        kernel,
        [classes],
        (rows // step,),
        [whole(tokens.shape), whole(gain.shape), whole(bias.shape), whole(weight.shape)],
        [tokens, gain, bias, weight],
        after,
        limit=20,
        out_specs=[whole_out((rows, width)), tile(step, width), tile(step, wide)],
        out_shape=[
            jax.ShapeDtypeStruct((rows, width), BF),
            in_hbm((rows, width), BF),
            jax.ShapeDtypeStruct((rows, wide), BF),
        ],
        cost_estimate=cost(2 * rows * width * wide, 2 * rows * (3 * width + wide) + 2 * weight.size),
    )


def self_attend(qkv, classes, after=()):
    clips = classes.shape[0]
    rows, wide = qkv.shape
    width = wide // 3

    def kernel(cls_ref, qkv_ref, o_ref):
        clip = pl.program_id(0)
        start = start_dyn(cls_ref, clip, clips)

        def body(count, live):
            at = pl.ds(start, count)

            def load(part):
                def get(head):
                    pair = pair_of(head)
                    return qkv_ref[at, part * width + pair.start : part * width + pair.stop]

                return get

            def store(head, mixed):
                o_ref[at, pair_of(head)] = mixed

            attend(load(0), load(1), load(2), store, live)

        by_class(cls_ref[clip], body)

        @pl.when(clip == clips - 1)
        def _():
            clear_tail(cls_ref, clips, [o_ref])

    return call(
        kernel,
        [classes],
        (clips,),
        [whole(qkv.shape)],
        [qkv],
        after,
        limit=20,
        out_specs=whole_out((rows, width)),
        out_shape=jax.ShapeDtypeStruct((rows, width), BF),
        cost_estimate=cost(16 * rows * MOST * width, 2 * rows * (wide + width)),
    )


def feed_forward(x, mixed, classes, gains, biases, w_out, w_up, w_down, w_fq, step, tiles, done=None, after=()):
    clips = classes.shape[0]
    rows, width = x.shape
    hidden = w_up.shape[1]
    chunk = width
    first, last = tiles
    shapes = [(width, F32), (width, BF), (hidden, BF), (hidden, BF), (width, F32), (width, BF), (width, BF)]
    count = 0 if done is None else len(shapes)

    def kernel(cls_ref, x_ref, o_ref, gain_ref, bias_ref, out_w, up_w, down_w, fq_w, *refs):
        mid_ref, h_ref, u_ref, act_ref, layer_ref, n_ref, fq_ref, part_ref = refs[count:]
        live = (first + pl.program_id(0)) * step < total_of(cls_ref, clips)

        @pl.when(live)
        def _():
            middle = x_ref[...].astype(F32) + dot(o_ref[...], out_w[...], 1, 0)
            mid_ref[...] = middle
            unit, _ = norm_stats(middle)
            low = (unit * gain_ref[:, width : 2 * width] + bias_ref[:, width : 2 * width]).astype(BF)
            h_ref[...] = low
            layer = middle
            for at in range(0, hidden, chunk):
                part = slice(at, at + chunk)
                up = dot(low, up_w[:, part], 1, 0)
                inner = jnp.tanh(GELU_A * (up + GELU_B * (up * up * up)))
                act = (0.5 * up * (1.0 + inner)).astype(BF)
                u_ref[:, part] = up.astype(BF)
                act_ref[:, part] = act
                layer = layer + dot(act, down_w[part, :], 1, 0)
            layer_ref[...] = layer
            unit, _ = norm_stats(layer)
            low = (unit * gain_ref[:, 2 * width :] + bias_ref[:, 2 * width :]).astype(BF)
            n_ref[...] = low
            part_ref[...] = low
            fq_ref[...] = dot(low, fq_w[...], 1, 0).astype(BF)

        @pl.when(jnp.logical_not(live))
        def _():
            for ref in (mid_ref, h_ref, u_ref, act_ref, layer_ref, n_ref, fq_ref, part_ref):
                ref[...] = jnp.zeros_like(ref)

    weights = [w_out, w_up, w_down, w_fq]
    operands = [classes, x, mixed, gains, biases, *weights] + list(done or [])
    share = (last - first) * step

    def part_tile(columns):
        return pl.BlockSpec((step, columns), lambda i, *_: (first + i, 0))

    return call(
        kernel,
        operands[:1],
        (last - first,),
        [part_tile(width), part_tile(width), whole(gains.shape), whole(biases.shape)]
            + [whole(w.shape) for w in weights]
            + [pl.BlockSpec(memory_space=pl.ANY)] * count,
        operands[1:],
        after,
        limit=20,
        out_specs=[part_tile(columns) for columns, _ in shapes] + [tile(step, width)],
        out_shape=[in_hbm((rows, columns), kind) for columns, kind in shapes] + [in_hbm((share, width), BF)],
        input_output_aliases={len(operands) - count + i: i for i in range(count)},
        cost_estimate=cost(
            2 * share * sum(w.size for w in weights),
            2 * sum(w.size for w in weights) + share * (4 * 5 * width + 4 * hidden),
        ),
    )


def join_attend(arrived, fq, grad_mixed, w_kv, classes, first, last, after=()):
    clips = classes.shape[0]
    rows, width = fq.shape
    wide = w_kv.shape[1]
    parts = len(arrived)
    share = (last - first) * MOST

    def kernel(cls_ref, *refs):
        pieces = refs[:parts]
        q_ref, do_ref, kv_w, o_ref, dq_ref, dn_ref, dkv_ref = refs[parts : parts + 7]
        kv = refs[-1]
        n_ref = refs[parts + 7] if parts > 1 else pieces[0]
        clip = first + pl.program_id(0)
        start = start_dyn(cls_ref, clip, clips)
        base = start_of(cls_ref, first)

        if parts > 1:

            @pl.when(clip == first)
            def _():
                at = 0
                for piece in pieces:
                    n_ref[at : at + piece.shape[0], :] = piece[...]
                    at += piece.shape[0]

        def body(count, live):
            at = pl.ds(start, count)
            to = pl.ds(pl.multiple_of(start - base, 16), count)
            kv[:count, :] = dot(n_ref[at, :], kv_w[...], 1, 0).astype(BF)

            def load_k(head):
                return kv[:count, pair_of(head)]

            def load_v(head):
                pair = pair_of(head)
                return kv[:count, width + pair.start : width + pair.stop]

            def store(head, query, key, value, mixed):
                pair = pair_of(head)
                o_ref[to, pair] = mixed
                dq_ref[to, pair] = query
                dkv_ref[to, pair] = key
                dkv_ref[to, width + pair.start : width + pair.stop] = value

            attend_back(
                lambda head: q_ref[at, pair_of(head)],
                load_k,
                load_v,
                lambda head: do_ref[at, pair_of(head)],
                None,
                store,
                live,
            )
            dn_ref[to, :] = dot(dkv_ref[to, :], kv_w[...], 1, 1).astype(BF)

        by_class(cls_ref[clip], body)

        @pl.when(clip == last - 1)
        def _():
            clear_from(start_of(cls_ref, last) - base, [o_ref, dq_ref, dkv_ref, dn_ref])

    operands = [*arrived, fq, grad_mixed, w_kv]
    return call(
        kernel,
        [classes],
        (last - first,),
        [whole(v.shape) for v in operands],
        [*operands],
        after,
        limit=24,
        out_specs=[whole_out((share, width))] * (4 if parts == 1 else 5),
        scratch=[pltpu.VMEM((MOST, wide), BF)],
        out_shape=[
            in_hbm((share, width), BF), in_hbm((share, width), BF), jax.ShapeDtypeStruct((share, width), BF),
            in_hbm((share, wide), BF),
        ]
        + ([in_hbm((rows, width), BF)] if parts > 1 else []),
        cost_estimate=cost(32 * rows * MOST * width, 10 * rows * width),
    )


def join_weights(own, products, classes, shards, order, after=()):
    clips = classes.shape[0]
    flat, places = [], []

    def place(value):
        for at, held in enumerate(flat):
            if held is value:
                return at
        flat.append(value)
        return len(flat) - 1

    for left, right, column in products:
        places.append(([place(v) for v in left], [place(v) for v in right], column))
    width = products[0][0][0].shape[1]
    share = min(v.shape[0] for v in flat)
    specs, shapes = part_outs(shards, width // shards, width, [0, len(products)], 0)

    def kernel(cls_ref, own_ref, *refs):
        kept, sent, acc = refs[-3:]
        index = pl.program_id(0)
        tail = pl.ds(start_of(cls_ref, clips // 2), share)

        def pieces(at, column):
            part = slice(column * width, (column + 1) * width)
            if len(at) == 2:
                return refs[at[0]][:, part], refs[at[1]][:, part]
            return refs[at[0]][:share, part], refs[at[0]][tail, part]

        for block, (left, right, column) in enumerate(places):

            @pl.when(index == block)
            def _():
                left_head, left_tail = pieces(left, 0)
                right_head, right_tail = pieces(right, column)
                acc[...] = (dot(left_head, right_head, 0, 0) + dot(left_tail, right_tail, 0, 0)).astype(BF)

        put_parts(acc, own_ref[0], shards, order, kept, sent)

    out = call(
        kernel,
        [classes, own],
        (len(products),),
        [whole(v.shape) for v in flat],
        flat,
        after,
        limit=24,
        out_specs=specs,
        scratch=[pltpu.VMEM((width, width), BF)],
        out_shape=shapes,
        cost_estimate=cost(2 * share * width * width, 4 * share * width),
    )
    return Sum(*out, order)


def join_result(layer, mixed, w_out, classes, slots, after=()):
    clips = classes.shape[0]
    rows, width = layer.shape

    def kernel(cls_ref, layer_ref, oa, ob, w_ref, out_ref):
        for clip in range(clips):
            start = start_of(cls_ref, clip)
            o_ref = oa if clip < clips // 2 else ob
            base = 0 if clip < clips // 2 else start_of(cls_ref, clips // 2)

            def body(count, live, start=start, base=base, o_ref=o_ref, clip=clip):
                at = pl.ds(start, count)
                from_at = pl.ds(pl.multiple_of(start - base, 16), count)
                value = layer_ref[at, :] + dot(o_ref[from_at, :], w_ref[...], 1, 0)
                held = min(count, SLOT)
                row = lax.broadcasted_iota(jnp.int32, value.shape, 0)
                value = jnp.where(row < live, value, 0.0).astype(BF)
                first = clip * SLOT
                out_ref[first : first + held, :] = value[:held]
                if held < SLOT:
                    out_ref[first + held : first + SLOT, :] = jnp.zeros((SLOT - held, width), BF)

            by_class(cls_ref[clip], body)

    return call(
        kernel,
        [classes],
        (1,),
        [whole(v.shape) for v in (layer, *mixed, w_out)],
        [layer, *mixed, w_out],
        after,
        limit=20,
        out_specs=whole_out((slots, width)),
        out_shape=jax.ShapeDtypeStruct((slots, width), BF),
        cost_estimate=cost(2 * rows * width * width, 8 * rows * width + 2 * w_out.size),
    )


def join_back(own, dfq, back, layer, grad, act, classes, gains, w_fq, step, shards, orders, cuts, after=()):
    clips = classes.shape[0]
    rows, width = layer.shape
    tall = act.shape[1]
    blocks = tall // width
    tiles = rows // step
    bounds = [*cuts, width]
    half = shards // 2
    outs_shapes = [
        jax.ShapeDtypeStruct((half, tall // shards, bounds[k + 1] - bounds[k]), BF) for k in range(len(orders)) for _ in range(2)
    ]

    def kernel(
        cls_ref, own_ref, dfqa, dfqb, backa, backb, layer_ref, g_ref, act_ref, gain_ref, fq_w,
        out_ref, gain_acc, bias_acc, *refs,
    ):
        outs = refs[:-4]
        dfq_ref, back_ref, low_ref, acc = refs[-4:]
        index = pl.program_id(0)

        @pl.when(index == 0)
        def _():
            gain_acc[...] = jnp.zeros_like(gain_acc)
            bias_acc[...] = jnp.zeros_like(bias_acc)
            base = start_of(cls_ref, clips // 2)
            merge(dfqa, dfqb, base, dfq_ref)
            merge(backa, backb, base, back_ref)

        total = total_of(cls_ref, clips)
        live = index * step < total
        at = pl.ds(pl.multiple_of(jnp.minimum(index, tiles - 1) * step, 16), step)

        @pl.when((index < tiles) & live)
        def _():
            grad_norm = dot(dfq_ref[at, :], fq_w[...], 1, 1) + back_ref[at, :].astype(F32)
            grad_layer = g_ref[...].astype(F32) + norm_back(
                layer_ref[...], gain_ref[:, 2 * width :], grad_norm, gain_acc, bias_acc
            )
            out_ref[...] = grad_layer
            low_ref[at, :] = grad_layer.astype(BF)

        @pl.when((index < tiles) & jnp.logical_not(live))
        def _():
            out_ref[...] = jnp.zeros_like(out_ref)
            low_ref[at, :] = jnp.zeros((step, width), BF)

        @pl.when(index >= tiles)
        def _():
            product_block(acc, act_ref, low_ref)
            put_parts_tall(acc, own_ref[0], orders, bounds, outs, index - tiles)

    def row_tile(columns):
        return pl.BlockSpec((step, columns), lambda i, *_: (jnp.minimum(i, tiles - 1), 0))

    out = call(
        kernel,
        [classes, own],
        (tiles + blocks,),
        [whole(v.shape) for v in (*dfq, *back)]
            + [row_tile(width)] * 2
            + [pl.BlockSpec((rows, width), lambda i, *_: (0, jnp.maximum(i - tiles, 0)))]
            + [whole(gains.shape), whole(w_fq.shape)],
        [*dfq, *back, layer, grad, act, gains, w_fq],
        after,
        limit=20,
        out_specs=[row_tile(width)] + [whole_out((1, width))] * 2 + [whole_out(v.shape) for v in outs_shapes],
            scratch=[pltpu.VMEM((rows, width), BF)] * 3 + [pltpu.VMEM((width, width), BF)],
        out_shape=[jax.ShapeDtypeStruct((rows, width), F32)]
        + [jax.ShapeDtypeStruct((1, width), F32)] * 2
        + outs_shapes,
        cost_estimate=cost(2 * rows * width * (width + tall), 16 * rows * width + 2 * act.size + 2 * tall * width),
    )
    return *out[:3], *(Sum(*out[3 + 2 * k : 5 + 2 * k], order) for k, order in enumerate(orders))


def feed_forward_back(grad_layer, up, middle, classes, gains, w_down, w_up, w_out, step, after=()):
    clips = classes.shape[0]
    rows, width = middle.shape
    hidden = w_up.shape[1]
    chunk = width
    blocks = hidden // width

    def kernel(
        cls_ref, g_ref, u_ref, mid_ref, gain_ref, down_w, up_w, out_w,
        gmid_ref, low_ref, do_ref, hid_ref, gain_acc, bias_acc,
    ):
        index = pl.program_id(0)

        @pl.when(index == 0)
        def _():
            gain_acc[...] = jnp.zeros_like(gain_acc)
            bias_acc[...] = jnp.zeros_like(bias_acc)

        live = index * step < total_of(cls_ref, clips)

        @pl.when(live)
        def _():
            grad_layer = g_ref[...]
            down_low = grad_layer.astype(BF)
            total_norm = [jnp.zeros((step, width), F32)]

            def act_stage(k, held):
                held["g"] = dot(down_low, down_w[k * chunk : (k + 1) * chunk, :], 1, 1)

            def slope_stage(k, held):
                part = slice(k * chunk, (k + 1) * chunk)
                value = u_ref[:, part].astype(F32)
                square = value * value
                inner = jnp.tanh(value * (GELU_A + (GELU_A * GELU_B) * square))
                slope = (0.5 + 0.5 * inner) + value * (1.0 - inner * inner) * (
                    0.5 * GELU_A + (1.5 * GELU_A * GELU_B) * square
                )
                held["l"] = (held.pop("g") * slope).astype(BF)
                hid_ref[:, part] = held["l"]

            def norm_stage(k, held):
                total_norm[0] += dot(held.pop("l"), up_w[:, k * chunk : (k + 1) * chunk], 1, 1)

            interleave([act_stage, slope_stage, norm_stage], blocks)
            grad_middle = grad_layer + norm_back(
                mid_ref[...], gain_ref[:, width : 2 * width], total_norm[0], gain_acc, bias_acc
            )
            gmid_ref[...] = grad_middle
            low = grad_middle.astype(BF)
            low_ref[...] = low
            do_ref[...] = dot(low, out_w[...], 1, 1).astype(BF)

        @pl.when(jnp.logical_not(live))
        def _():
            for ref in (gmid_ref, low_ref, do_ref, hid_ref):
                ref[...] = jnp.zeros_like(ref)

    weights = [w_down, w_up, w_out]
    return call(
        kernel,
        [classes],
        (rows // step,),
        [tile(step, width), tile(step, hidden), tile(step, width), whole(gains.shape)]
            + [whole(w.shape) for w in weights],
        [grad_layer, up, middle, gains, *weights],
        after,
        limit=22,
        out_specs=[tile(step, width)] * 3 + [tile(step, hidden)] + [whole_out((1, width))] * 2,
        out_shape=[
            in_hbm((rows, width), F32),
            in_hbm((rows, width), BF),
            jax.ShapeDtypeStruct((rows, width), BF),
            in_hbm((rows, hidden), BF),
        ]
        + [jax.ShapeDtypeStruct((1, width), F32)] * 2,
        cost_estimate=cost(2 * rows * sum(w.size for w in weights), 2 * sum(w.size for w in weights)),
    )


def feed_forward_weights(own, normed, hidden_low, mixed, out_low, shards, orders, cut, after=()):
    rows, width = normed.shape
    blocks = hidden_low.shape[1] // width
    bounds = [0, cut, blocks + 1][: len(orders)] + [blocks + 1]
    specs, shapes = part_outs(shards, width // shards, width, bounds, 0)

    def kernel(own_ref, n_ref, hid_ref, o_ref, low_ref, *refs):
        outs, acc = refs[:-1], refs[-1]
        block = pl.program_id(0)

        @pl.when(block < blocks)
        def _():
            product_block(acc, n_ref, hid_ref)

        @pl.when(block == blocks)
        def _():
            product_block(acc, o_ref, low_ref)

        for kind, order in enumerate(orders):

            @pl.when((block >= bounds[kind]) & (block < bounds[kind + 1]))
            def _():
                put_parts(acc, own_ref[0], shards, order, *outs[2 * kind : 2 * kind + 2])

    out = call(
        kernel,
        [own],
        (blocks + 1,),
        [
                whole(normed.shape),
                pl.BlockSpec((rows, width), lambda j, *_: (0, jnp.minimum(j, blocks - 1))),
                whole(mixed.shape),
                whole(out_low.shape),
            ],
        [normed, hidden_low, mixed, out_low],
        after,
        limit=20,
        out_specs=specs,
            scratch=[pltpu.VMEM((width, width), BF)],
        out_shape=shapes,
        cost_estimate=cost(2 * rows * width * width * (blocks + 1), 2 * rows * width * 8),
    )
    return [Sum(*out[2 * k : 2 * k + 2], order) for k, order in enumerate(orders)]


def self_attend_back(own, qkv, mixed, grad, normed, classes, shards, orders, cut, after=()):
    clips = classes.shape[0]
    rows, wide = qkv.shape
    width = wide // 3
    bounds = [0, cut, 3]
    specs, shapes = part_outs(shards, width // shards, width, bounds, clips)

    def kernel(cls_ref, own_ref, qkv_ref, o_ref, do_ref, n_ref, d_ref, *refs):
        outs = refs[:4]
        acc = refs[4]
        index = pl.program_id(0)

        @pl.when(index < clips)
        def _():
            clip = jnp.minimum(index, clips - 1)
            start = start_dyn(cls_ref, clip, clips)

            def body(count, live):
                at = pl.ds(start, count)

                def columns(part, head):
                    pair = pair_of(head)
                    return slice(part * width + pair.start, part * width + pair.stop)

                def load(part):
                    return lambda head: qkv_ref[at, columns(part, head)]

                def store(head, query, key, value, _):
                    for part, result in enumerate((query, key, value)):
                        d_ref[at, columns(part, head)] = result

                attend_back(
                    load(0),
                    load(1),
                    load(2),
                    lambda head: do_ref[at, pair_of(head)],
                    lambda head: o_ref[at, pair_of(head)],
                    store,
                    live,
                )

            by_class(cls_ref[clip], body)

        @pl.when(index == clips - 1)
        def _():
            clear_tail(cls_ref, clips, [d_ref])

        products = [(n_ref, d_ref.at[:, p * width : (p + 1) * width]) for p in range(3)]
        for block, (left, right) in enumerate(products):

            @pl.when(index == clips + block)
            def _():
                product_block(acc, left, right)
                kind = 0 if block < cut else 1
                put_parts(acc, own_ref[0], shards, orders[kind], *outs[2 * kind : 2 * kind + 2])

    operands = [qkv, mixed, grad, normed]
    out = call(
        kernel,
        [classes, own],
        (clips + 3,),
        [whole(v.shape) for v in operands],
        [*operands],
        after,
        limit=20,
        out_specs=[whole_out((rows, wide))] + specs,
            scratch=[pltpu.VMEM((width, width), BF)],
        out_shape=[jax.ShapeDtypeStruct((rows, wide), BF)] + shapes,
        cost_estimate=cost(48 * rows * MOST * width, 16 * rows * width),
    )
    return out[0], Sum(*out[1:3], orders[0]), Sum(*out[3:5], orders[1])


def norm_project_back(dqkv, x, gmid, classes, gain, weight, step, slots, after=()):
    clips = classes.shape[0]
    rows, width = x.shape
    wide = weight.shape[1]

    def kernel(cls_ref, d_ref, x_ref, gmid_ref, gain_ref, w_ref, out_ref, gain_one, bias_one, packed):
        index = pl.program_id(0)

        @pl.when(index == 0)
        def _():
            gain_one[...] = jnp.zeros_like(gain_one)
            bias_one[...] = jnp.zeros_like(bias_one)

        @pl.when(index * step < total_of(cls_ref, clips))
        def _():
            grad_norm = dot(d_ref[...], w_ref[...], 1, 1)
            at = pl.ds(pl.multiple_of(index * step, 16), step)
            packed[at, :] = gmid_ref[...] + norm_back(
                x_ref[...].astype(F32), gain_ref[:, :width], grad_norm, gain_one, bias_one
            )

        @pl.when(index == rows // step - 1)
        def _():
            for clip in range(clips):
                start = start_of(cls_ref, clip)

                def body(count, live):
                    value = packed[pl.ds(start, count), :]
                    held = min(count, SLOT)
                    first = clip * SLOT
                    out_ref[first : first + held, :] = value[:held]
                    if held < SLOT:
                        out_ref[first + held : first + SLOT, :] = jnp.zeros((SLOT - held, width), F32)

                by_class(cls_ref[clip], body)

    return call(
        kernel,
        [classes],
        (rows // step,),
        [
                tile(step, wide), tile(step, width), tile(step, width), whole(gain.shape), whole(weight.shape),
            ],
        [dqkv, x, gmid, gain, weight],
        after,
        limit=20,
        out_specs=[whole_out((slots, width))] + [whole_out((1, width))] * 2,
            scratch=[pltpu.VMEM((rows, width), F32)],
        out_shape=[jax.ShapeDtypeStruct((slots, width), F32)] + [jax.ShapeDtypeStruct((1, width), F32)] * 2,
        cost_estimate=cost(2 * rows * width * wide, rows * (10 * width + 2 * wide) + 2 * weight.size),
    )


def exchange(value, bit):
    count = lax.axis_size("dp")
    return lax.ppermute(value, "dp", [(i, i ^ (1 << bit)) for i in range(count)])


def tie(values, *before):
    return lax.optimization_barrier((values, before))[0]


class Sum:
    def __init__(self, kept, sent, order):
        self.kept, self.sent, self.order, self.step = kept, sent, order, 0
        self.got = None

    def start(self):
        self.got = exchange(self.sent, self.order[self.step])

    def add(self, *before, go=True):
        if self.step == len(self.order):
            return self.result
        kept, got, self.got = self.kept, self.got, None
        if before:
            kept, got = tie((kept, got), *before)
        self.step += 1
        if self.step == len(self.order):
            self.result = kept[0].astype(F32) + got[0].astype(F32)
            return self.result
        half = kept.shape[0] // 2
        self.sent = (kept[half:].astype(F32) + got[half:].astype(F32)).astype(kept.dtype)
        self.kept = (kept[:half].astype(F32) + got[:half].astype(F32)).astype(kept.dtype)
        if go:
            self.start()
        return self.sent, self.kept


def take_turns(sums, last):
    for one in sums:
        if one.got is None:
            one.start()
        else:
            last = one.add(last)
    return last


def shifted(value, axis, steps):
    count = lax.axis_size(axis)
    return lax.ppermute(value, axis, [(source, (source + steps) % count) for source in range(count)])


def per_device(
    tokens, item_class, norm_gain, norm_bias, attn_qkv, attn_out, mlp_up, mlp_down,
    join_query, join_keyval, join_output, cotangent,
):
    width = tokens.shape[2]
    slots = tokens.shape[1]
    clips = item_class.shape[0]
    rows = clips * MOST
    shards = lax.axis_size("dp")
    step, small_step = MOST, MOST * 2 // 3
    w_qkv, w_out, w_up, w_down = attn_qkv[0], attn_out[0], mlp_up[0], mlp_down[0]
    w_fq, w_fkv, w_fo = join_query[0], join_keyval[0], join_output[0]
    own = lax.axis_index("dp").astype(jnp.int32)[None]

    next_fkv = shifted(w_fkv, "view", -1)
    norm_gain, norm_bias = norm_gain.reshape(1, -1), norm_bias.reshape(1, -1)
    x, low_one, qkv = norm_project(tokens[0], item_class, rows, norm_gain, norm_bias, w_qkv, step)
    mixed = self_attend(qkv, item_class)
    tiles = rows // small_step
    args = (x, mixed, item_class, norm_gain, norm_bias, w_out, w_up, w_down, w_fq, small_step)
    *done, part_a = feed_forward(*args, (0, tiles // 2))
    arrived_a = shifted(part_a, "view", -1)
    *done, part_b = feed_forward(*args, (tiles // 2, tiles), done)
    arrived_b = shifted(part_b, "view", -1)
    middle, low_two, up, act, layer, low_three, fq = done
    grad, grad_mixed = pack_grad(cotangent[0], item_class, rows, w_fo, after=(part_b, arrived_a))

    bits = range(bits_of(shards))
    orders = tuple(bits), (*bits[1::-1], *bits[2:])
    half = clips // 2
    join_args = (fq, grad_mixed, next_fkv, item_class)
    mixed_a, dfq_a, back_a, dkv_a = join_attend((arrived_a,), *join_args, 0, half)
    returned_a = shifted(back_a, "view", 1)
    mixed_b, dfq_b, back_b, dkv_b, arrived = join_attend((arrived_a, arrived_b), *join_args, half, clips, after=back_a)
    returned_b = shifted(back_b, "view", 1)
    join_mixed, dfq = (mixed_a, mixed_b), (dfq_a, dfq_b)
    by_y, by_z = orders
    dkv, arrived = (in_main(dkv_a), in_main(dkv_b)), in_main(arrived)
    join_y = join_weights(
        own, [((arrived,), dkv, 0), ((arrived,), dkv, 1)], item_class, shards, by_y, after=returned_a
    )
    join_y.start()
    join_z = join_weights(
        own, [((low_three,), dfq, 0), (join_mixed, (grad,), 0)], item_class, shards, by_z,
        after=(join_y.kept, returned_b),
    )
    join_z.start()
    joined = join_result(layer, join_mixed, w_fo, item_class, slots, after=join_z.kept)
    grad_layer, gain_three, bias_three, down_y, down_z = join_back(
        own, dfq, (returned_a, returned_b), layer, grad, in_main(act), item_class, norm_gain, w_fq,
        step, shards, orders, (0, width // 2), after=joined,
    )
    down_y.start()
    down_z.start()
    last = [one.add(gain_three) for one in (join_y, join_z)]
    gmid, out_low, do_self, hidden_low, gain_two, bias_two = feed_forward_back(
        grad_layer, in_main(up), middle, item_class, norm_gain, w_down, w_up, w_out, small_step, after=last
    )
    last = [one.add(gain_two, go=False) for one in (join_y, join_z)]
    last += [one.add(gain_two) for one in (down_y, down_z)]
    up_y, up_z = feed_forward_weights(
        own, low_two, in_main(hidden_low), mixed, out_low, shards, orders, 3, after=last
    )
    up_y.start()
    up_z.start()
    join_y.start()
    dqkv, self_y, self_z = self_attend_back(
        own, qkv, mixed, do_self, low_one, item_class, shards, orders, 2, after=up_y.kept
    )
    self_y.start()
    self_z.start()
    last = join_y.add(self_y.kept)
    join_z.start()
    last = [one.add(last, go=False) for one in (down_y, down_z)]
    grad_tokens, gain_one, bias_one = norm_project_back(
        dqkv, x, gmid, item_class, norm_gain, w_qkv, step, slots, after=last
    )
    small = jnp.concatenate([gain_one, gain_two, gain_three, bias_one, bias_two, bias_three], 0)
    small = small.reshape(6, shards, width // shards).transpose(1, 0, 2)
    small = jnp.stack([small[own[0] ^ place_to_part(place, tuple(bits))] for place in range(shards)])
    small = Sum(small[: shards // 2], small[shards // 2 :], tuple(bits))
    last = take_turns(
        (up_z, up_y, join_z, down_y, self_z, self_y, down_y, down_z, up_z, up_y, self_z, self_y, down_z), gain_one
    )
    small.sent = tie(small.sent, last)
    last = take_turns((small, up_z, small, up_y, small, self_z, self_y, small), last)
    for _ in bits[3:]:
        last = [one.add() for one in (join_y, join_z, down_y, down_z, up_y, up_z, self_y, self_z, small)]
    sum_fkv = shifted(tie(join_y.result, gain_one), "view", 1)
    return (
        joined[None],
        grad_tokens[None],
        small.result[None, :3],
        small.result[None, 3:],
        jnp.concatenate([self_y.result, self_z.result], 1)[None],
        up_z.result[None, :, width:],
        jnp.concatenate([up_y.result, up_z.result[:, :width]], 1)[None],
        jnp.concatenate([down_y.result, down_z.result], 1)[None],
        join_z.result[None, :, :width],
        sum_fkv[None],
        join_z.result[None, :, width:],
    )


def solution(mesh):
    weight = P("view", None, None)
    tokens = P("view", "dp", None)
    small = P("view", None, "dp")
    return jax.shard_map(
        per_device,
        mesh=mesh,
        in_specs=(tokens, P("dp")) + (weight,) * 9 + (tokens,),
        out_specs=(tokens, tokens, small, small) + (tokens,) * 7,
        check_vma=False,
    )
```
